1024 devices in a mesh: dp: 64 (over y, z_lo, core), slot: 4 (over z_hi), grp: 4 (over x).
Axes of the slice: x: 4, y: 8, z: 16 (z_hi: 4, z_lo: 4; z = z_hi * 4 + z_lo), core: 2. Of those that a mesh axis runs over, the one named last changes fastest.
Arguments:
- pooled: bfloat16 [2048, 512, 128], P(('dp', 'grp'), 'slot'), may hold values from -6 to 6
- cotangent: bfloat16 [2048, 512, 128], P(('dp', 'grp'), 'slot'), may hold values from -6 to 6
- compress_weight: bfloat16 [2, 512, 512], replicated, may hold values from -0.25 to 0.25
- fm_basis: bfloat16 [2, 512, 32], replicated, may hold values from -0.25 to 0.25
- fm_output: bfloat16 [2, 32, 128], replicated, may hold values from -0.09375 to 0.09375
- norm_gain: float32 [2, 128], replicated, may hold values from 0.5 to 1.5
- bag_ids: int32 [2048, 512, 8], P(('dp', 'grp'), 'slot'), may hold values from 0 to 4095
- bag_lengths: int32 [2048, 512], P(('dp', 'grp'), 'slot'), may hold values from 1 to 8
- slot_table: int32 [512], P('slot'), may hold values from 0 to 127, as said below
- table_home: int32 [128], replicated, may hold values from 0 to 127, as said below
Outputs:
- table_grad: float32 [128, 4096, 128], P('dp', ('slot', 'grp'))
The draws below stay inside these ranges and needn't reach their ends.
Inputs may be any that keep to these rules, and one draw needn't show every extreme that they name: `slot_table`: within each aligned block of 128 slots, at most 4 slots use tables whose table_home lies in one aligned block of 2 positions, and in every block of slots some block of positions takes exactly 4. `table_home`: A permutation: each position holds one table.
All inputs are finite; a program needn't handle non-finite values.
Results may differ from the reference program's by a relative error of at most 0.024.
Values may be sent and summed in bfloat16 or wider, within the bound.
No kernel may reach another device: no remote copies, remote signals or barrier semaphores. Data moves between devices by JAX's collectives and lax.ppermute only.
A program may use at most 64 MiB of HBM per device.

```python
import jax
import jax.numpy as jnp
from jax import lax

D = 128
SLOTS = 512
RANK = 32
LAYERS = 2
SAMPLE_DEV = 8
ROWS = 4096
TABLE_DEV = 2
BAG = 8
SLOT_DEV = 128
SAMPLES = 2048
TABLES = 128
CAPACITY = 4
N_SLOT = 4


def home_order(key):
    return jax.random.permutation(key, TABLES).astype(jnp.int32)


def draw_table_home(key, part):
    return home_order(key)


def draw_slot_table(key, part):
    placing = home_order(key)
    key = jax.random.fold_in(key, 7)
    inverse = jnp.argsort(placing).astype(jnp.int32)
    owner_count = TABLES // TABLE_DEV
    shard_count = SLOTS // SLOT_DEV

    def shard_draw(shard_key):
        sub_keys = jax.random.split(shard_key, 4)
        crowded = jax.random.randint(sub_keys[0], (), 0, owner_count).astype(jnp.int32)
        seat_list = jax.random.permutation(sub_keys[1], (owner_count - 1) * CAPACITY)[:SLOT_DEV - CAPACITY]
        others = (seat_list // CAPACITY).astype(jnp.int32)
        others = others + (others >= crowded).astype(jnp.int32)
        owners = jnp.concatenate([jnp.full((CAPACITY,), crowded, jnp.int32), others])
        owners = jax.random.permutation(sub_keys[2], owners)
        chosen = owners * TABLE_DEV + jax.random.randint(sub_keys[3], (SLOT_DEV,), 0, TABLE_DEV).astype(jnp.int32)
        return inverse[chosen]
    return jax.vmap(shard_draw)(jax.random.split(key, shard_count)).reshape(-1).astype(jnp.int32)


def plant(values, rng, low, high):
    index_at = [jax.random.randint(jax.random.fold_in(rng, axis), (), 0, length) for axis, length in enumerate(values.shape)]
    widest = values.shape.index(max(values.shape))
    beside = index_at[:widest] + [(index_at[widest] + 1) % values.shape[widest]] + index_at[widest + 1:]
    return values.at[tuple(index_at)].set(low).at[tuple(beside)].set(high)


def block_scale(key, shape, pieces, low, high):
    factor_of, own = 1.0, jax.random.fold_in(key, 6)
    for position, blocks in pieces:
        heights = jnp.exp(jax.random.uniform(jax.random.fold_in(own, position), (blocks,), jnp.float32, low / len(pieces), high / len(pieces)))
        factor_of = factor_of * jnp.repeat(heights, shape[position] // blocks).reshape([-1 if axis == position else 1 for axis in range(len(shape))])
    return factor_of


def noise(key, dims, deviation, bound, cuts=(), kind=jnp.bfloat16):
    factor_of = block_scale(key, dims, cuts, -0.22, 0.18) if cuts else 1.0
    values = jax.random.normal(key, dims, jnp.float32) * deviation * factor_of
    return jnp.minimum(jnp.maximum(values, -bound), bound).astype(kind)


def setup_inputs(seed: int = 0) -> dict:
    arg_keys = jax.random.split(jax.random.key(seed), 11)
    return {
        "pooled": noise(arg_keys[0], (SAMPLES, SLOTS, D), 1.0, 6.0, ((0, 256), (1, 4))),
        "cotangent": noise(arg_keys[1], (SAMPLES, SLOTS, D), 1.0, 6.0, ((0, 256), (1, 4))),
        "compress_weight": noise(arg_keys[2], (LAYERS, SLOTS, SLOTS), SLOTS ** -0.5, 0.25),
        "fm_basis": noise(arg_keys[3], (LAYERS, SLOTS, RANK), SLOTS ** -0.5, 0.25),
        "fm_output": noise(arg_keys[4], (LAYERS, RANK, D), (RANK * D) ** -0.5, 0.09375),
        "norm_gain": jnp.clip(1.0 + 0.1 * jax.random.normal(arg_keys[5], (LAYERS, D), jnp.float32), 0.5, 1.5),
        "bag_ids": plant(jax.random.randint(arg_keys[6], (SAMPLES, SLOTS, BAG), 0, ROWS), jax.random.fold_in(arg_keys[6], 1), 0, ROWS - 1).astype(jnp.int32),
        "bag_lengths": plant(jax.random.randint(arg_keys[7], (SAMPLES, SLOTS), 1, BAG + 1), jax.random.fold_in(arg_keys[7], 1), 1, BAG).astype(jnp.int32),
        "slot_table": draw_slot_table(jax.random.fold_in(arg_keys[10], 71), 0),
        "table_home": draw_table_home(jax.random.fold_in(arg_keys[10], 71), 0),
    }


norm_eps = 1e-05

def rounded(value):
    return lax.optimization_barrier(value.astype(jnp.bfloat16))

def norm_rows(total_sum):
    mean_value = lax.optimization_barrier(jnp.mean(total_sum, axis=-1, keepdims=True))
    centered = total_sum - mean_value
    variance = lax.optimization_barrier(jnp.mean(centered * centered, axis=-1, keepdims=True))
    inv_std = lax.rsqrt(variance + norm_eps)
    return (centered * inv_std, inv_std)

def layer_forward(inputs, compress, basis_map, output_map, gain_row):
    wide_in = inputs.astype(jnp.float32)
    coefficient = rounded(jnp.einsum('bnd,nk->bdk', wide_in, basis_map.astype(jnp.float32)))
    feature = rounded(jnp.einsum('bnd,bdk->bnk', wide_in, coefficient.astype(jnp.float32)))
    mixed_rows = jnp.einsum('sn,bnd->bsd', compress.astype(jnp.float32), wide_in)
    total_sum = wide_in + jnp.einsum('bnk,kd->bnd', feature.astype(jnp.float32), output_map.astype(jnp.float32)) + mixed_rows
    normed, inv_std = norm_rows(total_sum)
    return ((normed * gain_row).astype(jnp.bfloat16), normed, inv_std, coefficient)

def layer_backward(upstream, inputs, normed, inv_std, coefficient, compress, basis_map, output_map, gain_row):
    scaled = upstream.astype(jnp.float32) * gain_row
    grad_sum = inv_std * (scaled - lax.optimization_barrier(jnp.mean(scaled, axis=-1, keepdims=True)) - normed * lax.optimization_barrier(jnp.mean(scaled * normed, axis=-1, keepdims=True)))
    grad_low = rounded(grad_sum).astype(jnp.float32)
    grad_feat = rounded(jnp.einsum('bnd,kd->bnk', grad_low, output_map.astype(jnp.float32))).astype(jnp.float32)
    local_part = grad_sum + jnp.einsum('bnk,bdk->bnd', grad_feat, coefficient.astype(jnp.float32))
    sample_count = inputs.shape[0]
    low_blocks = grad_low.reshape(sample_count, N_SLOT, SLOT_DEV, D)
    feat_blocks = grad_feat.reshape(sample_count, N_SLOT, SLOT_DEV, RANK)
    input_blocks = inputs.astype(jnp.float32).reshape(sample_count, N_SLOT, SLOT_DEV, D)
    weight_blocks = compress.astype(jnp.float32).reshape(N_SLOT, SLOT_DEV, SLOTS)
    linear = jnp.einsum('ksn,bksd->kbnd', weight_blocks, low_blocks)
    grad_coeff = jnp.einsum('bksd,bksq->kbdq', input_blocks, feat_blocks)
    basis_part = jnp.einsum('nq,kbdq->kbnd', basis_map.astype(jnp.float32), grad_coeff, precision=lax.Precision.HIGHEST)
    slot_back = lax.optimization_barrier(jnp.sum(rounded(linear + basis_part).astype(jnp.float32), axis=0))
    return (local_part + slot_back).astype(jnp.bfloat16)

def reference(pooled, cotangent, compress_weight, fm_basis, fm_output, norm_gain, bag_ids, bag_lengths, slot_table, table_home):
    blocks = SAMPLES // SAMPLE_DEV
    positions = table_home[slot_table].astype(jnp.int32)

    def block_step(totals, block_entry):
        inputs, upstream, id_block, length_block = block_entry
        saved_list = []
        current = inputs
        for layer_id in range(LAYERS):
            result, normed, inv_std, coefficient = layer_forward(current, compress_weight[layer_id], fm_basis[layer_id], fm_output[layer_id], norm_gain[layer_id])
            saved_list.append((current, normed, inv_std, coefficient))
            current = result
        for layer_id in reversed(range(LAYERS)):
            layer_in, normed, inv_std, coefficient = saved_list[layer_id]
            upstream = layer_backward(upstream, layer_in, normed, inv_std, coefficient, compress_weight[layer_id], fm_basis[layer_id], fm_output[layer_id], norm_gain[layer_id])
        row_keys = positions[None, :, None] * ROWS + id_block
        is_live = jnp.arange(BAG, dtype=jnp.int32)[None, None, :] < length_block[:, :, None]
        target = jnp.where(is_live, row_keys, TABLES * ROWS).astype(jnp.int32)
        values = jnp.broadcast_to(upstream.astype(jnp.float32)[:, :, None, :], (SAMPLE_DEV, SLOTS, BAG, D))
        totals = totals.at[target.reshape(-1)].add(values.reshape(-1, D), mode='drop')
        return (totals, None)
    entries = (pooled.reshape(blocks, SAMPLE_DEV, SLOTS, D), cotangent.reshape(blocks, SAMPLE_DEV, SLOTS, D), bag_ids.reshape(blocks, SAMPLE_DEV, SLOTS, BAG), bag_lengths.reshape(blocks, SAMPLE_DEV, SLOTS))
    totals = jnp.zeros((TABLES * ROWS, D), jnp.float32)
    totals, unused_out = lax.scan(block_step, totals, entries)
    return totals.reshape(TABLES, ROWS, D)
```

```python
import jax
import jax.numpy as jnp
from jax import lax
from jax.experimental import pallas as pl
from jax.experimental.pallas import tpu as pltpu
from jax.sharding import PartitionSpec as P

D = 128
LAYERS = 2
ROWS = 4096
TABLE_DEV = 2
BAG = 8
CAPACITY = 4
N_SLOT = 4
N_GRP = 4
DP = 64
SLOT_DEV = 128
SLOTS = 512
RANK = 32
PAIR = 2
ROW_BLOCK = 256
DEAD = 64
ID_ROWS = 32
MSG_ROWS = 2 * PAIR * SLOT_DEV + 48

norm_eps = 1e-05
f32 = jnp.float32
bf16 = jnp.bfloat16


def dot(a, b, ca=1, cb=0):
    return lax.dot_general(a, b, (((ca,), (cb,)), ((), ())), preferred_element_type=f32)


def iota(shape, dim):
    return lax.broadcasted_iota(jnp.int32, shape, dim)


def layers_kernel(x_ref, compress_ref, basis_ref, output_ref, gain_ref, out_ref):
    gain = gain_ref[...]
    pair_rows = PAIR * SLOT_DEV
    current = []
    upstream = []
    for b in range(PAIR):
        rows = slice(b * SLOT_DEV, (b + 1) * SLOT_DEV)
        current.append(jnp.concatenate([x_ref[k, rows, :] for k in range(N_SLOT)], axis=0))
        rows = slice(pair_rows + b * SLOT_DEV, pair_rows + (b + 1) * SLOT_DEV)
        upstream.append(jnp.concatenate([x_ref[k, rows, :] for k in range(N_SLOT)], axis=0))
    saved = []
    for layer in range(LAYERS):
        wide = jnp.concatenate(current, axis=1)
        coefficient = dot(basis_ref[layer], wide, 0, 0).astype(bf16)
        mixed = dot(compress_ref[layer], wide)
        following = []
        entry = []
        for b in range(PAIR):
            lanes = slice(b * D, (b + 1) * D)
            coeff = coefficient[:, lanes]
            feature = dot(current[b], coeff, 1, 1).astype(bf16)
            total = current[b].astype(f32) + dot(feature, output_ref[layer]) + mixed[:, lanes]
            mean = jnp.mean(total, axis=1, keepdims=True)
            centered = total - mean
            variance = jnp.mean(centered * centered, axis=1, keepdims=True)
            inv_std = lax.rsqrt(variance + norm_eps)
            normed = centered * inv_std
            entry.append((current[b], normed, inv_std, coeff))
            following.append((normed * gain[layer : layer + 1]).astype(bf16))
        saved.append(entry)
        current = following
    for layer in reversed(range(LAYERS)):
        lows = []
        local = []
        grad_feats = []
        for b in range(PAIR):
            inputs, normed, inv_std, coeff = saved[layer][b]
            scaled = upstream[b].astype(f32) * gain[layer : layer + 1]
            grad_sum = inv_std * (
                scaled
                - jnp.mean(scaled, axis=1, keepdims=True)
                - normed * jnp.mean(scaled * normed, axis=1, keepdims=True)
            )
            low = grad_sum.astype(bf16)
            grad_feat = dot(low, output_ref[layer], 1, 1).astype(bf16)
            local.append(grad_sum + dot(grad_feat, coeff))
            lows.append(low)
            grad_feats.append(grad_feat)
        linear = dot(compress_ref[layer], jnp.concatenate(lows, axis=1), 0, 0)
        basis_twice = jnp.concatenate([basis_ref[layer], basis_ref[layer]], axis=1)
        for b in range(PAIR):
            grad_coeff = dot(grad_feats[b], saved[layer][b][0], 0, 0)
            high = grad_coeff.astype(bf16)
            rest = (grad_coeff - high.astype(f32)).astype(bf16)
            basis_part = dot(basis_twice, jnp.concatenate([high, rest], axis=0))
            upstream[b] = (local[b] + linear[:, b * D : (b + 1) * D] + basis_part).astype(bf16)
    shape = (DP * PAIR * CAPACITY, PAIR * SLOT_DEV)
    row = iota(shape, 0)
    row_key = row // (PAIR * CAPACITY) * CAPACITY + row % CAPACITY + row // CAPACITY % PAIR * 1024
    sample_key = iota((1, PAIR * SLOT_DEV), 1) // SLOT_DEV * 1024
    targets = []
    for k in range(N_SLOT):
        target = x_ref[k, 2 * pair_rows + ID_ROWS : 2 * pair_rows + ID_ROWS + 16, :]
        target = target[:1].astype(f32).astype(jnp.int32)
        targets.append(target)
        column_key = jnp.concatenate([target] * PAIR, axis=1) + sample_key
        placing = jnp.where(row_key == column_key, 1.0, 0.0).astype(bf16)
        rows = slice(k * SLOT_DEV, (k + 1) * SLOT_DEV)
        values = jnp.concatenate([u[rows] for u in upstream], axis=0)
        out_ref[:, k] = dot(placing, values).astype(bf16).reshape(DP, PAIR * CAPACITY, D)
    shape = (DP * 8, SLOTS)
    row = iota(shape, 0)
    row_key = row // 8 * CAPACITY + row % 8 * 1024
    column_key = jnp.concatenate([targets[k] + k * 1024 for k in range(N_SLOT)], axis=1)
    unpacked = []
    lane_in = iota((D, D), 0)
    lane_out = iota((D, D), 1)
    for k in range(N_SLOT):
        packed = x_ref[k, 2 * pair_rows : 2 * pair_rows + ID_ROWS, :]
        for q in range(D // ID_ROWS):
            spread = jnp.where(lane_in == q * 32 + lane_out % 32, 1.0, 0.0).astype(bf16)
            unpacked.append(dot(packed, spread).astype(bf16))
    unpacked = jnp.concatenate(unpacked, axis=0)
    rank_lane = iota((1, D), 1) // 32
    ids = jnp.zeros((DP * 8, D), f32)
    for rank in range(CAPACITY):
        placing = jnp.where(row_key + rank == column_key, 1.0, 0.0).astype(bf16)
        ids = ids + jnp.where(rank_lane == rank, dot(placing, unpacked), 0.0)
    out_ref[:, N_SLOT] = ids.astype(bf16).reshape(DP, 8, D)


def run_layers(messages, compress, basis, outputs, gain):
    return pl.pallas_call(
        layers_kernel,
        out_shape=jax.ShapeDtypeStruct((DP, N_SLOT + 1, 8, D), bf16),
        in_specs=[pl.BlockSpec(memory_space=pltpu.VMEM)] * 5,
        out_specs=pl.BlockSpec(memory_space=pltpu.VMEM),
        compiler_params=pltpu.CompilerParams(vmem_limit_bytes=48 << 20),
        cost_estimate=pl.CostEstimate(flops=2_000_000_000, bytes_accessed=4 << 20, transcendentals=4096),
        name="layers",
    )(messages, compress, basis, outputs, gain)


def bags_kernel(got_ref, out_ref, wide_ref, grads_ref, high_ref, low_ref):
    caps = N_SLOT * CAPACITY
    bags = PAIR * DP
    shape = (DP * 8, N_SLOT * bags)
    row = iota(shape, 0)
    lane = iota(shape, 1)
    pick = (row // 8 == lane % DP) & (row % 8 == lane // bags)
    ids = dot(
        got_ref[:, N_SLOT].reshape(DP * 8, D), jnp.where(pick, 1.0, 0.0).astype(bf16), 0, 0
    )
    first_sample = iota((1, bags), 1) < DP
    for k in range(N_SLOT):
        wide_ref[...] = got_ref[:, k].astype(f32).reshape(DP * 8, D)
        for rank in range(CAPACITY):
            cap = k * CAPACITY + rank
            both = ids[rank * 32 : (rank + 1) * 32, k * bags : (k + 1) * bags]
            own = jnp.where(first_sample, both[:16], both[16:])
            high, low = own[:8], own[8:]
            table = jnp.where(jnp.max(jnp.where(high >= DEAD, high - DEAD, high)[:1], axis=1, keepdims=True) >= 16, 1.0, 0.0)
            half = cap % 2
            lanes = slice(half * bags, (half + 1) * bags)
            high_ref[cap // 2, :, lanes] = high - 16.0 * table
            low_ref[cap // 2, :, lanes] = low
            values = jnp.concatenate(
                [wide_ref[pl.ds(b * CAPACITY + rank, DP, stride=8), :] for b in range(PAIR)], axis=0
            )
            rows = slice(half * bags, (half + 1) * bags)
            grads_ref[cap // 2, rows, :D] = (values * (1.0 - table)).astype(bf16)
            grads_ref[cap // 2, rows, D:] = (values * table).astype(bf16)
    rows_of = iota((ROW_BLOCK, 2 * bags), 0).astype(f32).astype(bf16)
    one = jnp.ones((), bf16)
    zero = jnp.zeros((), bf16)

    def block(index, carry):
        want = index.astype(f32)
        total = jnp.zeros((ROW_BLOCK, 2 * D), f32)
        for p in range(caps // 2):
            match = jnp.where(high_ref[p] == want, low_ref[p], -1.0)
            count = jnp.zeros((ROW_BLOCK, 2 * bags), bf16)
            for j in range(BAG):
                wanted = jnp.broadcast_to(match[j : j + 1], (16, 2 * bags)).astype(bf16)
                wanted = jnp.broadcast_to(wanted[None], (ROW_BLOCK // 16, 16, 2 * bags)).reshape(ROW_BLOCK, 2 * bags)
                count = count + jnp.where(rows_of == wanted, one, zero)
            total = total + dot(count, grads_ref[p])
        out_ref[index, 0] = total[:, :D].astype(bf16)
        out_ref[index, 1] = total[:, D:].astype(bf16)
        return carry

    lax.fori_loop(0, N_SLOT * N_GRP, block, 0)


def run_bags(got):
    pairs = N_SLOT * CAPACITY // 2
    return pl.pallas_call(
        bags_kernel,
        out_shape=jax.ShapeDtypeStruct((N_SLOT * N_GRP, TABLE_DEV, ROW_BLOCK, D), bf16),
        in_specs=[pl.BlockSpec(memory_space=pltpu.VMEM)],
        out_specs=pl.BlockSpec(memory_space=pltpu.VMEM),
        scratch_shapes=[
            pltpu.VMEM((DP * 8, D), f32),
            pltpu.VMEM((pairs, 2 * PAIR * DP, 2 * D), bf16),
            pltpu.VMEM((pairs, BAG, 2 * PAIR * DP), f32),
            pltpu.VMEM((pairs, BAG, 2 * PAIR * DP), f32),
        ],
        compiler_params=pltpu.CompilerParams(vmem_limit_bytes=48 << 20),
        cost_estimate=pl.CostEstimate(flops=20_000_000_000, bytes_accessed=4 << 20, transcendentals=0),
        name="bags",
    )(got)


def per_device(
    pooled,
    cotangent,
    compress_weight,
    fm_basis,
    fm_output,
    norm_gain,
    bag_ids,
    bag_lengths,
    slot_table,
    table_home,
):
    slot_count = pooled.shape[1]
    matches = slot_table[:, None] == jnp.arange(table_home.shape[0], dtype=jnp.int32)[None, :]
    position = jnp.sum(jnp.where(matches, table_home[None, :], 0), axis=1)
    owner = position // TABLE_DEV
    table = position % TABLE_DEV
    order = jnp.arange(slot_count, dtype=jnp.int32)
    rank = jnp.sum(
        ((owner[None, :] == owner[:, None]) & (order[None, :] < order[:, None])).astype(jnp.int32), axis=1
    )
    target = owner * CAPACITY + rank
    live = jnp.arange(BAG, dtype=jnp.int32)[None, None, :] < bag_lengths[:, :, None]
    high = jnp.where(live, bag_ids // ROW_BLOCK, DEAD) + table[None, :, None] * 16
    low = bag_ids % ROW_BLOCK
    parts = jnp.stack([high, low], axis=2).astype(bf16)
    parts = parts.reshape(N_SLOT, PAIR, 4, 32, 16).transpose(0, 3, 2, 1, 4).reshape(N_SLOT, ID_ROWS, D)
    marks = jnp.broadcast_to(target.astype(bf16)[None, None, :], (N_SLOT, 16, slot_count))
    messages = jnp.concatenate(
        [
            pooled.reshape(N_SLOT, PAIR * slot_count, D),
            cotangent.reshape(N_SLOT, PAIR * slot_count, D),
            parts,
            marks,
        ],
        axis=1,
    )
    messages = lax.all_to_all(messages, "slot", split_axis=0, concat_axis=0, tiled=True)
    sent = run_layers(messages, compress_weight, fm_basis, fm_output, norm_gain)
    got = lax.all_to_all(sent, "dp", split_axis=0, concat_axis=0, tiled=True)
    totals = run_bags(got)
    totals = totals.reshape(N_SLOT, N_GRP, TABLE_DEV, ROW_BLOCK, D).transpose(1, 0, 2, 3, 4)
    totals = lax.all_to_all(totals, "grp", split_axis=0, concat_axis=0, tiled=True)
    totals = jnp.sum(totals.astype(f32), axis=0).astype(bf16)
    totals = lax.all_to_all(totals, "slot", split_axis=0, concat_axis=0, tiled=True)
    return jnp.sum(totals.astype(f32), axis=0)


def solution(mesh):
    in_specs = (
        P(("dp", "grp"), "slot", None),
        P(("dp", "grp"), "slot", None),
        P(),
        P(),
        P(),
        P(),
        P(("dp", "grp"), "slot", None),
        P(("dp", "grp"), "slot"),
        P("slot"),
        P(),
    )
    out_specs = P("dp", ("slot", "grp"), None)
    return jax.shard_map(
        per_device, mesh=mesh, in_specs=in_specs, out_specs=out_specs, check_vma=False
    )
```

```python
import functools

import jax
import jax.numpy as jnp
from jax import lax
from jax.experimental import pallas as pl
from jax.experimental.pallas import tpu as pltpu
from jax.sharding import PartitionSpec as P

D = 128
LAYERS = 2
ROWS = 4096
TABLE_DEV = 2
BAG = 8
CAPACITY = 4
N_SLOT = 4
N_GRP = 4
DP = 64
SLOT_DEV = 128
SLOTS = 512
RANK = 32
PAIR = 2
ROW_BLOCK = 256
DEAD = 64
ID_ROWS = 32
MSG_ROWS = 2 * PAIR * SLOT_DEV + 48

norm_eps = 1e-05
f32 = jnp.float32
bf16 = jnp.bfloat16


def dot(a, b, ca=1, cb=0):
    return lax.dot_general(a, b, (((ca,), (cb,)), ((), ())), preferred_element_type=f32)


def iota(shape, dim):
    return lax.broadcasted_iota(jnp.int32, shape, dim)


def layers_kernel(x_ref, compress_ref, basis_ref, output_ref, gain_ref, out_ref):
    gain = gain_ref[...]
    pair_rows = PAIR * SLOT_DEV
    current = []
    upstream = []
    for b in range(PAIR):
        rows = slice(b * SLOT_DEV, (b + 1) * SLOT_DEV)
        current.append(jnp.concatenate([x_ref[k, rows, :] for k in range(N_SLOT)], axis=0))
        rows = slice(pair_rows + b * SLOT_DEV, pair_rows + (b + 1) * SLOT_DEV)
        upstream.append(jnp.concatenate([x_ref[k, rows, :] for k in range(N_SLOT)], axis=0))
    saved = []
    for layer in range(LAYERS):
        wide = jnp.concatenate(current, axis=1)
        coefficient = dot(basis_ref[layer], wide, 0, 0).astype(bf16)
        mixed = dot(compress_ref[layer], wide)
        following = []
        entry = []
        for b in range(PAIR):
            lanes = slice(b * D, (b + 1) * D)
            coeff = coefficient[:, lanes]
            feature = dot(current[b], coeff, 1, 1).astype(bf16)
            total = current[b].astype(f32) + dot(feature, output_ref[layer]) + mixed[:, lanes]
            mean = jnp.mean(total, axis=1, keepdims=True)
            centered = total - mean
            variance = jnp.mean(centered * centered, axis=1, keepdims=True)
            inv_std = lax.rsqrt(variance + norm_eps)
            normed = centered * inv_std
            entry.append((current[b], normed, inv_std, coeff))
            following.append((normed * gain[layer : layer + 1]).astype(bf16))
        saved.append(entry)
        current = following
    for layer in reversed(range(LAYERS)):
        lows = []
        local = []
        grad_feats = []
        for b in range(PAIR):
            inputs, normed, inv_std, coeff = saved[layer][b]
            scaled = upstream[b].astype(f32) * gain[layer : layer + 1]
            grad_sum = inv_std * (
                scaled
                - jnp.mean(scaled, axis=1, keepdims=True)
                - normed * jnp.mean(scaled * normed, axis=1, keepdims=True)
            )
            low = grad_sum.astype(bf16)
            grad_feat = dot(low, output_ref[layer], 1, 1).astype(bf16)
            local.append(grad_sum + dot(grad_feat, coeff))
            lows.append(low)
            grad_feats.append(grad_feat)
        linear = dot(compress_ref[layer], jnp.concatenate(lows, axis=1), 0, 0)
        basis_twice = jnp.concatenate([basis_ref[layer], basis_ref[layer]], axis=1)
        for b in range(PAIR):
            grad_coeff = dot(grad_feats[b], saved[layer][b][0], 0, 0)
            high = grad_coeff.astype(bf16)
            rest = (grad_coeff - high.astype(f32)).astype(bf16)
            basis_part = dot(basis_twice, jnp.concatenate([high, rest], axis=0))
            upstream[b] = (local[b] + linear[:, b * D : (b + 1) * D] + basis_part).astype(bf16)
    shape = (DP * PAIR * CAPACITY, PAIR * SLOT_DEV)
    row = iota(shape, 0)
    row_key = row // (PAIR * CAPACITY) * CAPACITY + row % CAPACITY + row // CAPACITY % PAIR * 1024
    sample_key = iota((1, PAIR * SLOT_DEV), 1) // SLOT_DEV * 1024
    targets = []
    for k in range(N_SLOT):
        target = x_ref[k, 2 * pair_rows + ID_ROWS : 2 * pair_rows + ID_ROWS + 16, :]
        target = target[:1].astype(f32).astype(jnp.int32)
        targets.append(target)
        column_key = jnp.concatenate([target] * PAIR, axis=1) + sample_key
        placing = jnp.where(row_key == column_key, 1.0, 0.0).astype(bf16)
        rows = slice(k * SLOT_DEV, (k + 1) * SLOT_DEV)
        values = jnp.concatenate([u[rows] for u in upstream], axis=0)
        out_ref[:, k] = dot(placing, values).astype(bf16).reshape(DP, PAIR * CAPACITY, D)
    shape = (DP * 8, SLOTS)
    row = iota(shape, 0)
    row_key = row // 8 * CAPACITY + row % 8 * 1024
    column_key = jnp.concatenate([targets[k] + k * 1024 for k in range(N_SLOT)], axis=1)
    unpacked = []
    lane_in = iota((D, D), 0)
    lane_out = iota((D, D), 1)
    for k in range(N_SLOT):
        packed = x_ref[k, 2 * pair_rows : 2 * pair_rows + ID_ROWS, :]
        for q in range(D // ID_ROWS):
            spread = jnp.where(lane_in == q * 32 + lane_out % 32, 1.0, 0.0).astype(bf16)
            unpacked.append(dot(packed, spread).astype(bf16))
    unpacked = jnp.concatenate(unpacked, axis=0)
    rank_lane = iota((1, D), 1) // 32
    ids = jnp.zeros((DP * 8, D), f32)
    for rank in range(CAPACITY):
        placing = jnp.where(row_key + rank == column_key, 1.0, 0.0).astype(bf16)
        ids = ids + jnp.where(rank_lane == rank, dot(placing, unpacked), 0.0)
    out_ref[:, N_SLOT] = ids.astype(bf16).reshape(DP, 8, D)


def run_layers(messages, compress, basis, outputs, gain):
    return pl.pallas_call(
        layers_kernel,
        out_shape=jax.ShapeDtypeStruct((DP, N_SLOT + 1, 8, D), bf16),
        in_specs=[pl.BlockSpec(memory_space=pltpu.VMEM)] * 5,
        out_specs=pl.BlockSpec(memory_space=pltpu.VMEM),
        compiler_params=pltpu.CompilerParams(vmem_limit_bytes=48 << 20),
        cost_estimate=pl.CostEstimate(flops=2_000_000_000, bytes_accessed=4 << 20, transcendentals=4096),
        name="layers",
    )(messages, compress, basis, outputs, gain)


def prepare_bags(got_ref, wide_ref, grads_ref, high_ref, low_ref):
    bags = PAIR * DP
    shape = (DP * 8, N_SLOT * bags)
    row = iota(shape, 0)
    lane = iota(shape, 1)
    pick = (row // 8 == lane % DP) & (row % 8 == lane // bags)
    ids = dot(
        got_ref[:, N_SLOT].reshape(DP * 8, D), jnp.where(pick, 1.0, 0.0).astype(bf16), 0, 0
    )
    first_sample = iota((1, bags), 1) < DP
    for k in range(N_SLOT):
        wide_ref[...] = got_ref[:, k].astype(f32).reshape(DP * 8, D)
        for rank in range(CAPACITY):
            cap = k * CAPACITY + rank
            both = ids[rank * 32 : (rank + 1) * 32, k * bags : (k + 1) * bags]
            own = jnp.where(first_sample, both[:16], both[16:])
            high, low = own[:8], own[8:]
            alive = jnp.where(high >= DEAD, high - DEAD, high)[:1]
            table = jnp.where(jnp.max(alive, axis=1, keepdims=True) >= 16, 1.0, 0.0)
            half = cap % 2
            lanes = slice(half * bags, (half + 1) * bags)
            high_ref[cap // 2, :, lanes] = high - 16.0 * table
            low_ref[cap // 2, :, lanes] = low
            values = jnp.concatenate(
                [wide_ref[pl.ds(b * CAPACITY + rank, DP, stride=8), :] for b in range(PAIR)], axis=0
            )
            rows = slice(half * bags, (half + 1) * bags)
            grads_ref[cap // 2, rows, :D] = (values * (1.0 - table)).astype(bf16)
            grads_ref[cap // 2, rows, D:] = (values * table).astype(bf16)


def add_rows(first, amount, shift, out_refs, grads_ref, high_ref, low_ref):
    lanes = 2 * PAIR * DP
    rows_of = (iota((amount, lanes), 0) + first).astype(f32).astype(bf16)
    one = jnp.ones((), bf16)
    zero = jnp.zeros((), bf16)

    def block(s, carry):
        for r in range(N_GRP):
            group = shift + r
            group = jnp.where(group >= N_GRP, group - N_GRP, group)
            want = (s * N_GRP + group).astype(f32)
            total = jnp.zeros((amount, 2 * D), f32)
            for p in range(N_SLOT * CAPACITY // 2):
                match = jnp.where(high_ref[p] == want, low_ref[p], -1.0)
                count = jnp.zeros((amount, lanes), bf16)
                for j in range(BAG):
                    wanted = jnp.broadcast_to(match[j : j + 1], (16, lanes)).astype(bf16)
                    wanted = jnp.broadcast_to(wanted[None], (amount // 16, 16, lanes)).reshape(amount, lanes)
                    count = count + jnp.where(rows_of == wanted, one, zero)
                total = total + dot(count, grads_ref[p])
            out_refs[r][s, 0] = total[:, :D].astype(bf16)
            out_refs[r][s, 1] = total[:, D:].astype(bf16)
        return carry

    lax.fori_loop(0, N_SLOT, block, 0)


def first_bags_kernel(amount, got_ref, out_ref, grads_ref, high_ref, low_ref, wide_ref):
    prepare_bags(got_ref, wide_ref, grads_ref, high_ref, low_ref)
    outs = [out_ref.at[r] for r in range(N_GRP)]
    add_rows(0, amount, jnp.int32(0), outs, grads_ref, high_ref, low_ref)


def second_bags_kernel(first, amount, shift_ref, grads_ref, high_ref, low_ref, *out_refs):
    add_rows(first, amount, shift_ref[0], out_refs, grads_ref, high_ref, low_ref)


VMEM_SPEC = pl.BlockSpec(memory_space=pltpu.VMEM)


def run_first_bags(got, amount):
    pairs = N_SLOT * CAPACITY // 2
    lanes = 2 * PAIR * DP
    return pl.pallas_call(
        functools.partial(first_bags_kernel, amount),
        out_shape=(
            jax.ShapeDtypeStruct((N_GRP, N_SLOT, TABLE_DEV, amount, D), bf16),
            jax.ShapeDtypeStruct((pairs, lanes, 2 * D), bf16),
            jax.ShapeDtypeStruct((pairs, BAG, lanes), f32),
            jax.ShapeDtypeStruct((pairs, BAG, lanes), f32),
        ),
        in_specs=[VMEM_SPEC],
        out_specs=(VMEM_SPEC,) * 4,
        scratch_shapes=[pltpu.VMEM((DP * 8, D), f32)],
        compiler_params=pltpu.CompilerParams(vmem_limit_bytes=32 << 20),
        cost_estimate=pl.CostEstimate(flops=10_000_000_000, bytes_accessed=4 << 20, transcendentals=0),
        name="first_bags",
    )(got)


def run_second_bags(shift, grads, high, low, first, amount):
    return pl.pallas_call(
        functools.partial(second_bags_kernel, first, amount),
        out_shape=(jax.ShapeDtypeStruct((N_SLOT, TABLE_DEV, amount, D), bf16),) * N_GRP,
        in_specs=[pl.BlockSpec(memory_space=pltpu.SMEM)] + [VMEM_SPEC] * 3,
        out_specs=(VMEM_SPEC,) * N_GRP,
        compiler_params=pltpu.CompilerParams(vmem_limit_bytes=32 << 20),
        cost_estimate=pl.CostEstimate(flops=10_000_000_000, bytes_accessed=4 << 20, transcendentals=0),
        name="second_bags",
    )(shift, grads, high, low)


def per_device(
    pooled,
    cotangent,
    compress_weight,
    fm_basis,
    fm_output,
    norm_gain,
    bag_ids,
    bag_lengths,
    slot_table,
    table_home,
):
    slot_count = pooled.shape[1]
    matches = slot_table[:, None] == jnp.arange(table_home.shape[0], dtype=jnp.int32)[None, :]
    position = jnp.sum(jnp.where(matches, table_home[None, :], 0), axis=1)
    owner = position // TABLE_DEV
    table = position % TABLE_DEV
    order = jnp.arange(slot_count, dtype=jnp.int32)
    rank = jnp.sum(
        ((owner[None, :] == owner[:, None]) & (order[None, :] < order[:, None])).astype(jnp.int32), axis=1
    )
    target = owner * CAPACITY + rank
    live = jnp.arange(BAG, dtype=jnp.int32)[None, None, :] < bag_lengths[:, :, None]
    high = jnp.where(live, bag_ids // ROW_BLOCK, DEAD) + table[None, :, None] * 16
    low = bag_ids % ROW_BLOCK
    parts = jnp.stack([high, low], axis=2).astype(bf16)
    parts = parts.reshape(N_SLOT, PAIR, 4, 32, 16).transpose(0, 3, 2, 1, 4).reshape(N_SLOT, ID_ROWS, D)
    marks = jnp.broadcast_to(target.astype(bf16)[None, None, :], (N_SLOT, 16, slot_count))
    messages = jnp.concatenate(
        [
            pooled.reshape(N_SLOT, PAIR * slot_count, D),
            cotangent.reshape(N_SLOT, PAIR * slot_count, D),
            parts,
            marks,
        ],
        axis=1,
    )
    messages = lax.all_to_all(messages, "slot", split_axis=0, concat_axis=0, tiled=True)
    sent = run_layers(messages, compress_weight, fm_basis, fm_output, norm_gain)
    got = lax.all_to_all(sent, "dp", split_axis=0, concat_axis=0, tiled=True)
    half = ROW_BLOCK // 2
    first, grads, high_ids, low_ids = run_first_bags(got, half)
    shift = lax.axis_index("grp").astype(jnp.int32).reshape(1)
    second = run_second_bags(shift, grads, high_ids, low_ids, half, half)
    first = lax.all_to_all(first, "grp", split_axis=0, concat_axis=0, tiled=True)
    first = jnp.sum(first.astype(f32), axis=0).astype(bf16)
    first, second = lax.optimization_barrier((first, second))
    first = lax.all_to_all(first, "slot", split_axis=0, concat_axis=0, tiled=True)
    pieces = [second[0]]
    for step in range(1, N_GRP):
        moves = [(i, (i + step) % N_GRP) for i in range(N_GRP)]
        pieces.append(lax.ppermute(second[step], "grp", moves))
    second = sum(piece.astype(f32) for piece in pieces).astype(bf16)
    second = lax.all_to_all(second, "slot", split_axis=0, concat_axis=0, tiled=True)
    return jnp.concatenate(
        [jnp.sum(first.astype(f32), axis=0), jnp.sum(second.astype(f32), axis=0)], axis=1
    )


def solution(mesh):
    in_specs = (
        P(("dp", "grp"), "slot", None),
        P(("dp", "grp"), "slot", None),
        P(),
        P(),
        P(),
        P(),
        P(("dp", "grp"), "slot", None),
        P(("dp", "grp"), "slot"),
        P("slot"),
        P(),
    )
    out_specs = P("dp", ("slot", "grp"), None)
    return jax.shard_map(
        per_device, mesh=mesh, in_specs=in_specs, out_specs=out_specs, check_vma=False
    )
```

```python
import functools

import jax
import jax.numpy as jnp
from jax import lax
from jax.experimental import pallas as pl
from jax.experimental.pallas import tpu as pltpu
from jax.sharding import PartitionSpec as P

D = 128
LAYERS = 2
ROWS = 4096
TABLE_DEV = 2
BAG = 8
CAPACITY = 4
N_SLOT = 4
N_GRP = 4
DP = 64
SLOT_DEV = 128
SLOTS = 512
RANK = 32
PAIR = 2
ROW_BLOCK = 256
DEAD = 64
ID_ROWS = 32
MSG_ROWS = 2 * PAIR * SLOT_DEV + 48

norm_eps = 1e-05
f32 = jnp.float32
bf16 = jnp.bfloat16


def dot(a, b, ca=1, cb=0):
    return lax.dot_general(a, b, (((ca,), (cb,)), ((), ())), preferred_element_type=f32)


def iota(shape, dim):
    return lax.broadcasted_iota(jnp.int32, shape, dim)


def layers_kernel(x_ref, compress_ref, basis_ref, output_ref, gain_ref, out_ref):
    gain = gain_ref[...]
    pair_rows = PAIR * SLOT_DEV
    current = []
    upstream = []
    for b in range(PAIR):
        rows = slice(b * SLOT_DEV, (b + 1) * SLOT_DEV)
        current.append(jnp.concatenate([x_ref[k, rows, :] for k in range(N_SLOT)], axis=0))
        rows = slice(pair_rows + b * SLOT_DEV, pair_rows + (b + 1) * SLOT_DEV)
        upstream.append(jnp.concatenate([x_ref[k, rows, :] for k in range(N_SLOT)], axis=0))
    saved = []
    for layer in range(LAYERS):
        wide = jnp.concatenate(current, axis=1)
        coefficient = dot(basis_ref[layer], wide, 0, 0).astype(bf16)
        mixed = dot(compress_ref[layer], wide)
        following = []
        entry = []
        for b in range(PAIR):
            lanes = slice(b * D, (b + 1) * D)
            coeff = coefficient[:, lanes]
            feature = dot(current[b], coeff, 1, 1).astype(bf16)
            total = current[b].astype(f32) + dot(feature, output_ref[layer]) + mixed[:, lanes]
            mean = jnp.mean(total, axis=1, keepdims=True)
            centered = total - mean
            variance = jnp.mean(centered * centered, axis=1, keepdims=True)
            inv_std = lax.rsqrt(variance + norm_eps)
            normed = centered * inv_std
            entry.append((current[b], normed, inv_std, coeff))
            following.append((normed * gain[layer : layer + 1]).astype(bf16))
        saved.append(entry)
        current = following
    for layer in reversed(range(LAYERS)):
        lows = []
        local = []
        grad_feats = []
        for b in range(PAIR):
            inputs, normed, inv_std, coeff = saved[layer][b]
            scaled = upstream[b].astype(f32) * gain[layer : layer + 1]
            grad_sum = inv_std * (
                scaled
                - jnp.mean(scaled, axis=1, keepdims=True)
                - normed * jnp.mean(scaled * normed, axis=1, keepdims=True)
            )
            low = grad_sum.astype(bf16)
            grad_feat = dot(low, output_ref[layer], 1, 1).astype(bf16)
            local.append(grad_sum + dot(grad_feat, coeff))
            lows.append(low)
            grad_feats.append(grad_feat)
        linear = dot(compress_ref[layer], jnp.concatenate(lows, axis=1), 0, 0)
        basis_twice = jnp.concatenate([basis_ref[layer], basis_ref[layer]], axis=1)
        for b in range(PAIR):
            grad_coeff = dot(grad_feats[b], saved[layer][b][0], 0, 0)
            high = grad_coeff.astype(bf16)
            rest = (grad_coeff - high.astype(f32)).astype(bf16)
            basis_part = dot(basis_twice, jnp.concatenate([high, rest], axis=0))
            upstream[b] = (local[b] + linear[:, b * D : (b + 1) * D] + basis_part).astype(bf16)
    shape = (DP * PAIR * CAPACITY, PAIR * SLOT_DEV)
    row = iota(shape, 0)
    row_key = row // (PAIR * CAPACITY) * CAPACITY + row % CAPACITY + row // CAPACITY % PAIR * 1024
    sample_key = iota((1, PAIR * SLOT_DEV), 1) // SLOT_DEV * 1024
    targets = []
    for k in range(N_SLOT):
        target = x_ref[k, 2 * pair_rows + ID_ROWS : 2 * pair_rows + ID_ROWS + 16, :]
        target = target[:1].astype(f32).astype(jnp.int32)
        targets.append(target)
        column_key = jnp.concatenate([target] * PAIR, axis=1) + sample_key
        placing = jnp.where(row_key == column_key, 1.0, 0.0).astype(bf16)
        rows = slice(k * SLOT_DEV, (k + 1) * SLOT_DEV)
        values = jnp.concatenate([u[rows] for u in upstream], axis=0)
        out_ref[:, k] = dot(placing, values).astype(bf16).reshape(DP, PAIR * CAPACITY, D)
    shape = (DP * 8, SLOTS)
    row = iota(shape, 0)
    row_key = row // 8 * CAPACITY + row % 8 * 1024
    column_key = jnp.concatenate([targets[k] + k * 1024 for k in range(N_SLOT)], axis=1)
    unpacked = []
    lane_in = iota((D, D), 0)
    lane_out = iota((D, D), 1)
    for k in range(N_SLOT):
        packed = x_ref[k, 2 * pair_rows : 2 * pair_rows + ID_ROWS, :]
        for q in range(D // ID_ROWS):
            spread = jnp.where(lane_in == q * 32 + lane_out % 32, 1.0, 0.0).astype(bf16)
            unpacked.append(dot(packed, spread).astype(bf16))
    unpacked = jnp.concatenate(unpacked, axis=0)
    rank_lane = iota((1, D), 1) // 32
    ids = jnp.zeros((DP * 8, D), f32)
    for rank in range(CAPACITY):
        placing = jnp.where(row_key + rank == column_key, 1.0, 0.0).astype(bf16)
        ids = ids + jnp.where(rank_lane == rank, dot(placing, unpacked), 0.0)
    out_ref[:, N_SLOT] = ids.astype(bf16).reshape(DP, 8, D)


def run_layers(messages, compress, basis, outputs, gain):
    return pl.pallas_call(
        layers_kernel,
        out_shape=jax.ShapeDtypeStruct((DP, N_SLOT + 1, 8, D), bf16),
        in_specs=[pl.BlockSpec(memory_space=pltpu.VMEM)] * 5,
        out_specs=pl.BlockSpec(memory_space=pltpu.VMEM),
        compiler_params=pltpu.CompilerParams(vmem_limit_bytes=48 << 20),
        cost_estimate=pl.CostEstimate(flops=2_000_000_000, bytes_accessed=4 << 20, transcendentals=4096),
        name="layers",
    )(messages, compress, basis, outputs, gain)


def prepare_bags(got_ref, wide_ref, grads_ref, high_ref, low_ref):
    bags = PAIR * DP
    shape = (DP * 8, N_SLOT * bags)
    row = iota(shape, 0)
    lane = iota(shape, 1)
    pick = (row // 8 == lane % DP) & (row % 8 == lane // bags)
    ids = dot(
        got_ref[:, N_SLOT].reshape(DP * 8, D), jnp.where(pick, 1.0, 0.0).astype(bf16), 0, 0
    )
    first_sample = iota((1, bags), 1) < DP
    for k in range(N_SLOT):
        wide_ref[...] = got_ref[:, k].astype(f32).reshape(DP * 8, D)
        for rank in range(CAPACITY):
            cap = k * CAPACITY + rank
            both = ids[rank * 32 : (rank + 1) * 32, k * bags : (k + 1) * bags]
            own = jnp.where(first_sample, both[:16], both[16:])
            high, low = own[:8], own[8:]
            alive = jnp.where(high >= DEAD, high - DEAD, high)[:1]
            table = jnp.where(jnp.max(alive, axis=1, keepdims=True) >= 16, 1.0, 0.0)
            half = cap % 2
            lanes = slice(half * bags, (half + 1) * bags)
            high_ref[cap // 2, :, lanes] = high - 16.0 * table
            low_ref[cap // 2, :, lanes] = low
            values = jnp.concatenate(
                [wide_ref[pl.ds(b * CAPACITY + rank, DP, stride=8), :] for b in range(PAIR)], axis=0
            )
            rows = slice(half * bags, (half + 1) * bags)
            grads_ref[cap // 2, rows, :D] = (values * (1.0 - table)).astype(bf16)
            grads_ref[cap // 2, rows, D:] = (values * table).astype(bf16)


def add_rows(first, amount, groups, out_ref, grads_ref, high_ref, low_ref):
    lanes = 2 * PAIR * DP
    rows_of = (iota((amount, lanes), 0) + first).astype(f32).astype(bf16)
    one = jnp.ones((), bf16)
    zero = jnp.zeros((), bf16)

    def block(s, carry):
        for r, group in enumerate(groups):
            want = (s * N_GRP + group).astype(f32)
            total = jnp.zeros((amount, 2 * D), f32)
            for p in range(N_SLOT * CAPACITY // 2):
                match = jnp.where(high_ref[p] == want, low_ref[p], -1.0)
                count = jnp.zeros((amount, lanes), bf16)
                for j in range(BAG):
                    wanted = jnp.broadcast_to(match[j : j + 1], (16, lanes)).astype(bf16)
                    wanted = jnp.broadcast_to(wanted[None], (amount // 16, 16, lanes)).reshape(amount, lanes)
                    count = count + jnp.where(rows_of == wanted, one, zero)
                total = total + dot(count, grads_ref[p])
            out_ref[r, s, 0] = total[:, :D].astype(bf16)
            out_ref[r, s, 1] = total[:, D:].astype(bf16)
        return carry

    lax.fori_loop(0, N_SLOT, block, 0)


def first_bags_kernel(amount, groups_ref, got_ref, out_ref, grads_ref, high_ref, low_ref, wide_ref):
    prepare_bags(got_ref, wide_ref, grads_ref, high_ref, low_ref)
    groups = [groups_ref[0], groups_ref[1]]
    add_rows(0, amount, groups, out_ref, grads_ref, high_ref, low_ref)


def later_bags_kernel(first, amount, groups_ref, grads_ref, high_ref, low_ref, out_ref):
    groups = [groups_ref[0], groups_ref[1]]
    add_rows(first, amount, groups, out_ref, grads_ref, high_ref, low_ref)


VMEM_SPEC = pl.BlockSpec(memory_space=pltpu.VMEM)
SMEM_SPEC = pl.BlockSpec(memory_space=pltpu.SMEM)
BAGS_COST = pl.CostEstimate(flops=200_000_000, bytes_accessed=1 << 20, transcendentals=0)
ADD_COST = pl.CostEstimate(flops=1_000_000, bytes_accessed=1 << 20, transcendentals=0)


def part_shape(amount):
    return jax.ShapeDtypeStruct((2, N_SLOT, TABLE_DEV, amount, D), bf16)


def run_first_bags(groups, got, amount):
    pairs = N_SLOT * CAPACITY // 2
    lanes = 2 * PAIR * DP
    return pl.pallas_call(
        functools.partial(first_bags_kernel, amount),
        out_shape=(
            part_shape(amount),
            jax.ShapeDtypeStruct((pairs, lanes, 2 * D), bf16),
            jax.ShapeDtypeStruct((pairs, BAG, lanes), f32),
            jax.ShapeDtypeStruct((pairs, BAG, lanes), f32),
        ),
        in_specs=[SMEM_SPEC, VMEM_SPEC],
        out_specs=(VMEM_SPEC,) * 4,
        scratch_shapes=[pltpu.VMEM((DP * 8, D), f32)],
        compiler_params=pltpu.CompilerParams(vmem_limit_bytes=32 << 20),
        cost_estimate=BAGS_COST,
        name="first_bags",
    )(groups, got)


def run_later_bags(groups, prepared, first, amount, name):
    return pl.pallas_call(
        functools.partial(later_bags_kernel, first, amount),
        out_shape=part_shape(amount),
        in_specs=[SMEM_SPEC] + [VMEM_SPEC] * 3,
        out_specs=VMEM_SPEC,
        compiler_params=pltpu.CompilerParams(vmem_limit_bytes=32 << 20),
        cost_estimate=BAGS_COST,
        name=name,
    )(groups, *prepared)


def add_parts_kernel(kept_ref, got_ref, own_ref, sent_ref):
    for s in range(N_SLOT):
        own_ref[s] = (kept_ref[0, s].astype(f32) + got_ref[0, s].astype(f32)).astype(bf16)
        sent_ref[s] = (kept_ref[1, s].astype(f32) + got_ref[1, s].astype(f32)).astype(bf16)


def add_parts(kept, got, name):
    one = jax.ShapeDtypeStruct(kept.shape[1:], bf16)
    return pl.pallas_call(
        add_parts_kernel,
        out_shape=(one, one),
        in_specs=[VMEM_SPEC] * 2,
        out_specs=(VMEM_SPEC,) * 2,
        compiler_params=pltpu.CompilerParams(vmem_limit_bytes=8 << 20),
        cost_estimate=ADD_COST,
        name=name,
    )(kept, got)


def join_kernel(low_ref, low_last_ref, high_ref, high_last_ref, out_ref):
    for s in range(N_SLOT):
        out_ref[s, 0] = (low_ref[s].astype(f32) + low_last_ref[s].astype(f32)).astype(bf16)
        out_ref[s, 1] = (high_ref[s].astype(f32) + high_last_ref[s].astype(f32)).astype(bf16)


def join_parts(*parts):
    shape = (parts[0].shape[0], 2, *parts[0].shape[1:])
    return pl.pallas_call(
        join_kernel,
        out_shape=jax.ShapeDtypeStruct(shape, bf16),
        in_specs=[VMEM_SPEC] * 4,
        out_specs=VMEM_SPEC,
        compiler_params=pltpu.CompilerParams(vmem_limit_bytes=8 << 20),
        cost_estimate=ADD_COST,
        name="join_parts",
    )(*parts)


def final_kernel(got_ref, out_ref):
    for half in range(2):
        for t in range(TABLE_DEV):
            total = got_ref[0, half, t].astype(f32)
            for s in range(1, N_SLOT):
                total = total + got_ref[s, half, t].astype(f32)
            out_ref[t, half] = total


def final_sum(got):
    return pl.pallas_call(
        final_kernel,
        out_shape=jax.ShapeDtypeStruct((TABLE_DEV, 2, ROW_BLOCK // 2, D), f32),
        in_specs=[VMEM_SPEC],
        out_specs=VMEM_SPEC,
        compiler_params=pltpu.CompilerParams(vmem_limit_bytes=8 << 20),
        cost_estimate=ADD_COST,
        name="final_sum",
    )(got)


def per_device(
    pooled,
    cotangent,
    compress_weight,
    fm_basis,
    fm_output,
    norm_gain,
    bag_ids,
    bag_lengths,
    slot_table,
    table_home,
):
    slot_count = pooled.shape[1]
    matches = slot_table[:, None] == jnp.arange(table_home.shape[0], dtype=jnp.int32)[None, :]
    position = jnp.sum(jnp.where(matches, table_home[None, :], 0), axis=1)
    owner = position // TABLE_DEV
    table = position % TABLE_DEV
    order = jnp.arange(slot_count, dtype=jnp.int32)
    rank = jnp.sum(
        ((owner[None, :] == owner[:, None]) & (order[None, :] < order[:, None])).astype(jnp.int32), axis=1
    )
    target = owner * CAPACITY + rank
    live = jnp.arange(BAG, dtype=jnp.int32)[None, None, :] < bag_lengths[:, :, None]
    high = jnp.where(live, bag_ids // ROW_BLOCK, DEAD) + table[None, :, None] * 16
    low = bag_ids % ROW_BLOCK
    parts = jnp.stack([high, low], axis=2).astype(bf16)
    parts = parts.reshape(N_SLOT, PAIR, 4, 32, 16).transpose(0, 3, 2, 1, 4).reshape(N_SLOT, ID_ROWS, D)
    marks = jnp.broadcast_to(target.astype(bf16)[None, None, :], (N_SLOT, 16, slot_count))
    messages = jnp.concatenate(
        [
            pooled.reshape(N_SLOT, PAIR * slot_count, D),
            cotangent.reshape(N_SLOT, PAIR * slot_count, D),
            parts,
            marks,
        ],
        axis=1,
    )
    messages = lax.all_to_all(messages, "slot", split_axis=0, concat_axis=0, tiled=True)
    sent = run_layers(messages, compress_weight, fm_basis, fm_output, norm_gain)
    got = lax.all_to_all(sent, "dp", split_axis=0, concat_axis=0, tiled=True)
    half = ROW_BLOCK // 2
    me = lax.axis_index("grp").astype(jnp.int32)
    side = me ^ 1
    mirror = N_GRP - 1 - me
    across = side ^ 3
    side_moves = [(i, i ^ 1) for i in range(N_GRP)]
    mirror_moves = [(i, N_GRP - 1 - i) for i in range(N_GRP)]
    low_sent, *prepared = run_first_bags(jnp.stack([side, across]), got, half)
    low_got = lax.ppermute(low_sent, "grp", side_moves)
    high_sent = run_later_bags(jnp.stack([mirror, across]), prepared, half, half, "high_sent")
    high_got = lax.ppermute(high_sent, "grp", mirror_moves)
    low_kept = run_later_bags(jnp.stack([me, mirror]), prepared, 0, half, "low_kept")
    low, low_next = add_parts(low_kept, low_got, "low_parts")
    low_last = lax.ppermute(low_next, "grp", mirror_moves)
    high_kept = run_later_bags(jnp.stack([me, side]), prepared, half, half, "high_kept")
    high, high_next = add_parts(high_kept, high_got, "high_parts")
    high_last = lax.ppermute(high_next, "grp", side_moves)
    totals = join_parts(low, low_last, high, high_last)
    totals = lax.all_to_all(totals, "slot", split_axis=0, concat_axis=0, tiled=True)
    return final_sum(totals).reshape(TABLE_DEV, ROW_BLOCK, D)


def solution(mesh):
    in_specs = (
        P(("dp", "grp"), "slot", None),
        P(("dp", "grp"), "slot", None),
        P(),
        P(),
        P(),
        P(),
        P(("dp", "grp"), "slot", None),
        P(("dp", "grp"), "slot"),
        P("slot"),
        P(),
    )
    out_specs = P("dp", ("slot", "grp"), None)
    return jax.shard_map(
        per_device, mesh=mesh, in_specs=in_specs, out_specs=out_specs, check_vma=False
    )
```

```python
import functools

import jax
import jax.numpy as jnp
from jax import lax
from jax.experimental import pallas as pl
from jax.experimental.pallas import tpu as pltpu
from jax.sharding import PartitionSpec as P

D = 128
LAYERS = 2
ROWS = 4096
TABLE_DEV = 2
BAG = 8
CAPACITY = 4
N_SLOT = 4
N_GRP = 4
DP = 64
SLOT_DEV = 128
SLOTS = 512
RANK = 32
PAIR = 2
ROW_BLOCK = 256
DEAD = 64
ID_ROWS = 32
MSG_ROWS = 2 * PAIR * SLOT_DEV + 48

norm_eps = 1e-05
f32 = jnp.float32
bf16 = jnp.bfloat16


def dot(a, b, ca=1, cb=0):
    return lax.dot_general(a, b, (((ca,), (cb,)), ((), ())), preferred_element_type=f32)


def iota(shape, dim):
    return lax.broadcasted_iota(jnp.int32, shape, dim)


def layers_kernel(x_ref, compress_ref, basis_ref, output_ref, gain_ref, out_ref):
    gain = gain_ref[...]
    pair_rows = PAIR * SLOT_DEV
    current = []
    upstream = []
    for b in range(PAIR):
        rows = slice(b * SLOT_DEV, (b + 1) * SLOT_DEV)
        current.append(jnp.concatenate([x_ref[k, rows, :] for k in range(N_SLOT)], axis=0))
        rows = slice(pair_rows + b * SLOT_DEV, pair_rows + (b + 1) * SLOT_DEV)
        upstream.append(jnp.concatenate([x_ref[k, rows, :] for k in range(N_SLOT)], axis=0))
    saved = []
    for layer in range(LAYERS):
        wide = jnp.concatenate(current, axis=1)
        coefficient = dot(basis_ref[layer], wide, 0, 0).astype(bf16)
        mixed = dot(compress_ref[layer], wide)
        following = []
        entry = []
        for b in range(PAIR):
            lanes = slice(b * D, (b + 1) * D)
            coeff = coefficient[:, lanes]
            feature = dot(current[b], coeff, 1, 1).astype(bf16)
            total = current[b].astype(f32) + dot(feature, output_ref[layer]) + mixed[:, lanes]
            mean = jnp.mean(total, axis=1, keepdims=True)
            centered = total - mean
            variance = jnp.mean(centered * centered, axis=1, keepdims=True)
            inv_std = lax.rsqrt(variance + norm_eps)
            normed = centered * inv_std
            entry.append((current[b], normed, inv_std, coeff))
            following.append((normed * gain[layer : layer + 1]).astype(bf16))
        saved.append(entry)
        current = following
    for layer in reversed(range(LAYERS)):
        lows = []
        local = []
        grad_feats = []
        for b in range(PAIR):
            inputs, normed, inv_std, coeff = saved[layer][b]
            scaled = upstream[b].astype(f32) * gain[layer : layer + 1]
            grad_sum = inv_std * (
                scaled
                - jnp.mean(scaled, axis=1, keepdims=True)
                - normed * jnp.mean(scaled * normed, axis=1, keepdims=True)
            )
            low = grad_sum.astype(bf16)
            grad_feat = dot(low, output_ref[layer], 1, 1).astype(bf16)
            local.append(grad_sum + dot(grad_feat, coeff))
            lows.append(low)
            grad_feats.append(grad_feat)
        linear = dot(compress_ref[layer], jnp.concatenate(lows, axis=1), 0, 0)
        basis_twice = jnp.concatenate([basis_ref[layer], basis_ref[layer]], axis=1)
        for b in range(PAIR):
            grad_coeff = dot(grad_feats[b], saved[layer][b][0], 0, 0)
            high = grad_coeff.astype(bf16)
            rest = (grad_coeff - high.astype(f32)).astype(bf16)
            basis_part = dot(basis_twice, jnp.concatenate([high, rest], axis=0))
            upstream[b] = (local[b] + linear[:, b * D : (b + 1) * D] + basis_part).astype(bf16)
    shape = (DP * PAIR * CAPACITY, PAIR * SLOT_DEV)
    row = iota(shape, 0)
    row_key = row // (PAIR * CAPACITY) * CAPACITY + row % CAPACITY + row // CAPACITY % PAIR * 1024
    sample_key = iota((1, PAIR * SLOT_DEV), 1) // SLOT_DEV * 1024
    targets = []
    for k in range(N_SLOT):
        target = x_ref[k, 2 * pair_rows + ID_ROWS : 2 * pair_rows + ID_ROWS + 16, :]
        target = target[:1].astype(f32).astype(jnp.int32)
        targets.append(target)
        column_key = jnp.concatenate([target] * PAIR, axis=1) + sample_key
        placing = jnp.where(row_key == column_key, 1.0, 0.0).astype(bf16)
        rows = slice(k * SLOT_DEV, (k + 1) * SLOT_DEV)
        values = jnp.concatenate([u[rows] for u in upstream], axis=0)
        out_ref[:, k] = dot(placing, values).astype(bf16).reshape(DP, PAIR * CAPACITY, D)
    shape = (DP * 8, SLOTS)
    row = iota(shape, 0)
    row_key = row // 8 * CAPACITY + row % 8 * 1024
    column_key = jnp.concatenate([targets[k] + k * 1024 for k in range(N_SLOT)], axis=1)
    unpacked = []
    lane_in = iota((D, D), 0)
    lane_out = iota((D, D), 1)
    for k in range(N_SLOT):
        packed = x_ref[k, 2 * pair_rows : 2 * pair_rows + ID_ROWS, :]
        for q in range(D // ID_ROWS):
            spread = jnp.where(lane_in == q * 32 + lane_out % 32, 1.0, 0.0).astype(bf16)
            unpacked.append(dot(packed, spread).astype(bf16))
    unpacked = jnp.concatenate(unpacked, axis=0)
    rank_lane = iota((1, D), 1) // 32
    ids = jnp.zeros((DP * 8, D), f32)
    for rank in range(CAPACITY):
        placing = jnp.where(row_key + rank == column_key, 1.0, 0.0).astype(bf16)
        ids = ids + jnp.where(rank_lane == rank, dot(placing, unpacked), 0.0)
    out_ref[:, N_SLOT] = ids.astype(bf16).reshape(DP, 8, D)


def run_layers(messages, compress, basis, outputs, gain):
    return pl.pallas_call(
        layers_kernel,
        out_shape=jax.ShapeDtypeStruct((DP, N_SLOT + 1, 8, D), bf16),
        in_specs=[pl.BlockSpec(memory_space=pltpu.VMEM)] * 5,
        out_specs=pl.BlockSpec(memory_space=pltpu.VMEM),
        compiler_params=pltpu.CompilerParams(vmem_limit_bytes=48 << 20),
        cost_estimate=pl.CostEstimate(flops=2_000_000_000, bytes_accessed=4 << 20, transcendentals=4096),
        name="layers",
    )(messages, compress, basis, outputs, gain)


def prepare_bags(got_ref, wide_ref, grads_ref, high_ref, low_ref):
    bags = PAIR * DP
    shape = (DP * 8, N_SLOT * bags)
    row = iota(shape, 0)
    lane = iota(shape, 1)
    pick = (row // 8 == lane % DP) & (row % 8 == lane // bags)
    ids = dot(
        got_ref[:, N_SLOT].reshape(DP * 8, D), jnp.where(pick, 1.0, 0.0).astype(bf16), 0, 0
    )
    first_sample = iota((1, bags), 1) < DP
    for k in range(N_SLOT):
        wide_ref[...] = got_ref[:, k].astype(f32).reshape(DP * 8, D)
        for rank in range(CAPACITY):
            cap = k * CAPACITY + rank
            both = ids[rank * 32 : (rank + 1) * 32, k * bags : (k + 1) * bags]
            own = jnp.where(first_sample, both[:16], both[16:])
            high, low = own[:8], own[8:]
            alive = jnp.where(high >= DEAD, high - DEAD, high)[:1]
            table = jnp.where(jnp.max(alive, axis=1, keepdims=True) >= 16, 1.0, 0.0)
            half = cap % 2
            lanes = slice(half * bags, (half + 1) * bags)
            high_ref[cap // 2, :, lanes] = high - 16.0 * table
            low_ref[cap // 2, :, lanes] = low
            values = jnp.concatenate(
                [wide_ref[pl.ds(b * CAPACITY + rank, DP, stride=8), :] for b in range(PAIR)], axis=0
            )
            rows = slice(half * bags, (half + 1) * bags)
            grads_ref[cap // 2, rows, :D] = (values * (1.0 - table)).astype(bf16)
            grads_ref[cap // 2, rows, D:] = (values * table).astype(bf16)


def add_rows(blocks_ref, out_ref, grads_ref, high_ref, low_ref):
    lanes = 2 * PAIR * DP
    half = ROW_BLOCK // 2
    rows_of = iota((half, lanes), 0).astype(f32).astype(bf16)
    one = jnp.ones((), bf16)
    zero = jnp.zeros((), bf16)

    def block(index, carry):
        want = blocks_ref[index].astype(f32)
        for part in range(2):
            total = jnp.zeros((half, 2 * D), f32)
            for p in range(N_SLOT * CAPACITY // 2):
                match = jnp.where(high_ref[p] == want, low_ref[p] - float(part * half), -1.0)
                count = jnp.zeros((half, lanes), bf16)
                for j in range(BAG):
                    wanted = jnp.broadcast_to(match[j : j + 1], (16, lanes)).astype(bf16)
                    wanted = jnp.broadcast_to(wanted[None], (half // 16, 16, lanes)).reshape(half, lanes)
                    count = count + jnp.where(rows_of == wanted, one, zero)
                total = total + dot(count, grads_ref[p])
            rows = slice(part * half, (part + 1) * half)
            out_ref[index // 2, index % 2, 0, rows] = total[:, :D].astype(bf16)
            out_ref[index // 2, index % 2, 1, rows] = total[:, D:].astype(bf16)
        return carry

    lax.fori_loop(0, 4, block, 0)


def first_bags_kernel(blocks_ref, got_ref, out_ref, grads_ref, high_ref, low_ref, wide_ref):
    prepare_bags(got_ref, wide_ref, grads_ref, high_ref, low_ref)
    add_rows(blocks_ref, out_ref, grads_ref, high_ref, low_ref)


def later_bags_kernel(blocks_ref, grads_ref, high_ref, low_ref, out_ref):
    add_rows(blocks_ref, out_ref, grads_ref, high_ref, low_ref)


VMEM_SPEC = pl.BlockSpec(memory_space=pltpu.VMEM)
SMEM_SPEC = pl.BlockSpec(memory_space=pltpu.SMEM)
BAGS_COST = pl.CostEstimate(flops=200_000_000, bytes_accessed=1 << 20, transcendentals=0)
ADD_COST = pl.CostEstimate(flops=1_000_000, bytes_accessed=1 << 20, transcendentals=0)
CHUNK = (TABLE_DEV, ROW_BLOCK, D)


def run_first_bags(blocks, got):
    pairs = N_SLOT * CAPACITY // 2
    lanes = 2 * PAIR * DP
    return pl.pallas_call(
        first_bags_kernel,
        out_shape=(
            jax.ShapeDtypeStruct((2, 2, *CHUNK), bf16),
            jax.ShapeDtypeStruct((pairs, lanes, 2 * D), bf16),
            jax.ShapeDtypeStruct((pairs, BAG, lanes), f32),
            jax.ShapeDtypeStruct((pairs, BAG, lanes), f32),
        ),
        in_specs=[SMEM_SPEC, VMEM_SPEC],
        out_specs=(VMEM_SPEC,) * 4,
        scratch_shapes=[pltpu.VMEM((DP * 8, D), f32)],
        compiler_params=pltpu.CompilerParams(vmem_limit_bytes=24 << 20),
        cost_estimate=BAGS_COST,
        name="first_bags",
    )(blocks, got)


def run_later_bags(blocks, prepared, name):
    return pl.pallas_call(
        later_bags_kernel,
        out_shape=jax.ShapeDtypeStruct((2, 2, *CHUNK), bf16),
        in_specs=[SMEM_SPEC] + [VMEM_SPEC] * 3,
        out_specs=VMEM_SPEC,
        compiler_params=pltpu.CompilerParams(vmem_limit_bytes=24 << 20),
        cost_estimate=BAGS_COST,
        name=name,
    )(blocks, *prepared)


def wide_sum(*refs):
    total = refs[0][...].astype(f32)
    for ref in refs[1:]:
        total = total + ref[...].astype(f32)
    return total


def add_parts_kernel(kept_ref, got_ref, own_ref, sent_ref):
    own_ref[...] = wide_sum(kept_ref.at[0], got_ref.at[0]).astype(bf16)
    sent_ref[...] = wide_sum(kept_ref.at[1], got_ref.at[1]).astype(bf16)


def relay_kernel(own_ref, got_ref, up_ref, down_ref, near_ref):
    up_ref[...] = wide_sum(own_ref.at[0, 0], got_ref.at[0, 0]).astype(bf16)
    down_ref[...] = wide_sum(own_ref.at[0, 1], got_ref.at[0, 1]).astype(bf16)
    near_ref[...] = wide_sum(own_ref.at[1], got_ref.at[1]).astype(bf16)


def join_kernel(own_ref, got_ref, near_ref, up_ref, down_ref, kept_ref, right_ref, left_ref):
    kept_ref[...] = wide_sum(own_ref.at[0], got_ref.at[0])
    right_ref[0] = wide_sum(near_ref.at[0], up_ref).astype(bf16)
    right_ref[1] = near_ref[1]
    left_ref[0] = wide_sum(own_ref.at[1, 0], got_ref.at[1, 0]).astype(bf16)
    left_ref[1] = wide_sum(own_ref.at[1, 1], got_ref.at[1, 1], down_ref).astype(bf16)


def final_kernel(kept_ref, right_ref, left_ref, out_ref):
    out_ref[...] = wide_sum(kept_ref, right_ref, left_ref)


def small_call(kernel, name, shapes, *args):
    outs = tuple(jax.ShapeDtypeStruct(shape, dtype) for shape, dtype in shapes)
    return pl.pallas_call(
        kernel,
        out_shape=outs,
        in_specs=[VMEM_SPEC] * len(args),
        out_specs=(VMEM_SPEC,) * len(outs),
        compiler_params=pltpu.CompilerParams(vmem_limit_bytes=8 << 20),
        cost_estimate=ADD_COST,
        name=name,
    )(*args)


def per_device(
    pooled,
    cotangent,
    compress_weight,
    fm_basis,
    fm_output,
    norm_gain,
    bag_ids,
    bag_lengths,
    slot_table,
    table_home,
):
    slot_count = pooled.shape[1]
    matches = slot_table[:, None] == jnp.arange(table_home.shape[0], dtype=jnp.int32)[None, :]
    position = jnp.sum(jnp.where(matches, table_home[None, :], 0), axis=1)
    owner = position // TABLE_DEV
    table = position % TABLE_DEV
    order = jnp.arange(slot_count, dtype=jnp.int32)
    rank = jnp.sum(
        ((owner[None, :] == owner[:, None]) & (order[None, :] < order[:, None])).astype(jnp.int32), axis=1
    )
    target = owner * CAPACITY + rank
    live = jnp.arange(BAG, dtype=jnp.int32)[None, None, :] < bag_lengths[:, :, None]
    high = jnp.where(live, bag_ids // ROW_BLOCK, DEAD) + table[None, :, None] * 16
    low = bag_ids % ROW_BLOCK
    parts = jnp.stack([high, low], axis=2).astype(bf16)
    parts = parts.reshape(N_SLOT, PAIR, 4, 32, 16).transpose(0, 3, 2, 1, 4).reshape(N_SLOT, ID_ROWS, D)
    marks = jnp.broadcast_to(target.astype(bf16)[None, None, :], (N_SLOT, 16, slot_count))
    messages = jnp.concatenate(
        [
            pooled.reshape(N_SLOT, PAIR * slot_count, D),
            cotangent.reshape(N_SLOT, PAIR * slot_count, D),
            parts,
            marks,
        ],
        axis=1,
    )
    messages = lax.all_to_all(messages, "slot", split_axis=0, concat_axis=0, tiled=True)
    sent = run_layers(messages, compress_weight, fm_basis, fm_output, norm_gain)
    got = lax.all_to_all(sent, "dp", split_axis=0, concat_axis=0, tiled=True)
    me = lax.axis_index("grp").astype(jnp.int32)
    side = me ^ 1
    mirror = N_GRP - 1 - me
    across = side ^ 3
    here = lax.axis_index("slot").astype(jnp.int32)
    far, after, before = (here + 2) % N_SLOT, (here + 1) % N_SLOT, (here + 3) % N_SLOT

    def blocks(groups, chunks):
        return jnp.stack([chunk * N_GRP + group for group in groups for chunk in chunks])

    half_a, half_b = (far, after), (here, before)
    side_moves = [(i, i ^ 1) for i in range(N_GRP)]
    mirror_moves = [(i, N_GRP - 1 - i) for i in range(N_GRP)]
    up_moves = [(i, (i + 1) % N_SLOT) for i in range(N_SLOT)]
    down_moves = [(i, (i - 1) % N_SLOT) for i in range(N_SLOT)]
    a_sent, *prepared = run_first_bags(blocks((side, across), half_a), got)
    a_got = lax.ppermute(a_sent, "grp", side_moves)
    b_sent = run_later_bags(blocks((mirror, across), half_b), prepared, "b_sent")
    b_got = lax.ppermute(b_sent, "grp", mirror_moves)
    a_kept = run_later_bags(blocks((me, mirror), half_a), prepared, "a_kept")
    part = ((2, *CHUNK), bf16)
    a_own, a_next = small_call(add_parts_kernel, "add_a", (part, part), a_kept, a_got)
    a_last = lax.ppermute(a_next, "grp", mirror_moves)
    b_blocks, a_own = lax.optimization_barrier((blocks((me, side), half_b), a_own))
    b_kept = run_later_bags(b_blocks, prepared, "b_kept")
    b_own, b_next = small_call(add_parts_kernel, "add_b", (part, part), b_kept, b_got)
    b_last = lax.ppermute(b_next, "grp", side_moves)
    table = (CHUNK[1:], bf16)
    up, down, near = small_call(relay_kernel, "relay", (table, table, (CHUNK, bf16)), a_own, a_last)
    up = lax.ppermute(up, "slot", up_moves)
    down = lax.ppermute(down, "slot", down_moves)
    kept, right, left = small_call(
        join_kernel, "join", ((CHUNK, f32), (CHUNK, bf16), (CHUNK, bf16)), b_own, b_last, near, up, down
    )
    right = lax.ppermute(right, "slot", up_moves)
    left = lax.ppermute(left, "slot", down_moves)
    return small_call(final_kernel, "final_sum", ((CHUNK, f32),), kept, right, left)[0]


def solution(mesh):
    in_specs = (
        P(("dp", "grp"), "slot", None),
        P(("dp", "grp"), "slot", None),
        P(),
        P(),
        P(),
        P(),
        P(("dp", "grp"), "slot", None),
        P(("dp", "grp"), "slot"),
        P("slot"),
        P(),
    )
    out_specs = P("dp", ("slot", "grp"), None)
    return jax.shard_map(
        per_device, mesh=mesh, in_specs=in_specs, out_specs=out_specs, check_vma=False
    )
```

```python
import functools

import jax
import jax.numpy as jnp
from jax import lax
from jax.experimental import pallas as pl
from jax.experimental.pallas import tpu as pltpu
from jax.sharding import PartitionSpec as P

D = 128
LAYERS = 2
ROWS = 4096
TABLE_DEV = 2
BAG = 8
CAPACITY = 4
N_SLOT = 4
N_GRP = 4
DP = 64
SLOT_DEV = 128
SLOTS = 512
RANK = 32
PAIR = 2
ROW_BLOCK = 256
DEAD = 64
ID_ROWS = 32
POOLED_ROWS = PAIR * SLOT_DEV
MSG_ROWS = 2 * POOLED_ROWS + ID_ROWS + 16

norm_eps = 1e-05
f32 = jnp.float32
bf16 = jnp.bfloat16


VMEM_SPEC = pl.BlockSpec(memory_space=pltpu.VMEM)
SMEM_SPEC = pl.BlockSpec(memory_space=pltpu.SMEM)


def dot(a, b, ca=1, cb=0):
    return lax.dot_general(a, b, (((ca,), (cb,)), ((), ())), preferred_element_type=f32)


def iota(shape, dim):
    return lax.broadcasted_iota(jnp.int32, shape, dim)


def messages_kernel(
    here_ref, pooled_ref, cotangent_ref, ids_ref, lengths_ref, slot_ref, home_ref, *out_refs
):
    slots = slot_ref[...]
    hot = jnp.where(iota((SLOT_DEV, SLOT_DEV), 0) == slots, 1.0, 0.0).astype(bf16)
    homes = jnp.broadcast_to(home_ref[...].astype(f32), (8, SLOT_DEV)).astype(bf16)
    across = dot(homes, hot)[:1].astype(jnp.int32)
    down = dot(hot, homes, 0, 1)[:, :1].astype(jnp.int32)
    earlier = iota((SLOT_DEV, SLOT_DEV), 0) < iota((SLOT_DEV, SLOT_DEV), 1)
    same = (down // TABLE_DEV == across // TABLE_DEV) & earlier
    rank = jnp.sum(jnp.where(same, 1.0, 0.0), axis=0, keepdims=True)
    target = (across // TABLE_DEV * CAPACITY).astype(f32) + rank
    table = across % TABLE_DEV * 16
    marks = jnp.broadcast_to(target, (16, SLOT_DEV)).astype(bf16)
    entry = iota((BAG, SLOT_DEV), 0)
    for r, out_ref in enumerate(out_refs):
        dest = lax.rem(here_ref[0] + r, N_SLOT)
        out_ref[:POOLED_ROWS] = pooled_ref[dest]
        out_ref[POOLED_ROWS : 2 * POOLED_ROWS] = cotangent_ref[dest]
        parts = []
        for b in range(PAIR):
            ids = ids_ref[dest * PAIR + b]
            live = entry < lengths_ref[dest * PAIR + b]
            parts.append((jnp.where(live, ids // ROW_BLOCK, DEAD) + table).astype(f32))
            parts.append((ids % ROW_BLOCK).astype(f32))
        out_ref[2 * POOLED_ROWS : 2 * POOLED_ROWS + ID_ROWS] = jnp.concatenate(parts, axis=0).astype(bf16)
        out_ref[2 * POOLED_ROWS + ID_ROWS :] = marks


def make_messages(here, *args):
    message = jax.ShapeDtypeStruct((MSG_ROWS, D), bf16)
    return pl.pallas_call(
        messages_kernel,
        out_shape=(message,) * N_SLOT,
        in_specs=[SMEM_SPEC] + [VMEM_SPEC] * len(args),
        out_specs=(VMEM_SPEC,) * N_SLOT,
        compiler_params=pltpu.CompilerParams(vmem_limit_bytes=16 << 20),
        cost_estimate=pl.CostEstimate(flops=1_000_000, bytes_accessed=2 << 20, transcendentals=0),
        name="messages",
    )(here, *args)


def layers_kernel(
    here_ref, own_ref, before_ref, far_ref, after_ref, compress_ref, basis_ref, output_ref, gain_ref, out_ref, x_ref
):
    for r, ref in enumerate((own_ref, after_ref, far_ref, before_ref)):
        x_ref[lax.rem(here_ref[0] + r, N_SLOT)] = ref[...]
    gain = gain_ref[...]
    pair_rows = POOLED_ROWS
    current = []
    upstream = []
    for b in range(PAIR):
        rows = slice(b * SLOT_DEV, (b + 1) * SLOT_DEV)
        current.append(jnp.concatenate([x_ref[k, rows, :] for k in range(N_SLOT)], axis=0))
        rows = slice(pair_rows + b * SLOT_DEV, pair_rows + (b + 1) * SLOT_DEV)
        upstream.append(jnp.concatenate([x_ref[k, rows, :] for k in range(N_SLOT)], axis=0))
    saved = []
    for layer in range(LAYERS):
        wide = jnp.concatenate(current, axis=1)
        coefficient = dot(basis_ref[layer], wide, 0, 0).astype(bf16)
        mixed = dot(compress_ref[layer], wide)
        following = []
        entry = []
        for b in range(PAIR):
            lanes = slice(b * D, (b + 1) * D)
            coeff = coefficient[:, lanes]
            feature = dot(current[b], coeff, 1, 1).astype(bf16)
            total = current[b].astype(f32) + dot(feature, output_ref[layer]) + mixed[:, lanes]
            mean = jnp.mean(total, axis=1, keepdims=True)
            centered = total - mean
            variance = jnp.mean(centered * centered, axis=1, keepdims=True)
            inv_std = lax.rsqrt(variance + norm_eps)
            normed = centered * inv_std
            entry.append((current[b], normed, inv_std, coeff))
            following.append((normed * gain[layer : layer + 1]).astype(bf16))
        saved.append(entry)
        current = following
    for layer in reversed(range(LAYERS)):
        lows = []
        local = []
        grad_feats = []
        for b in range(PAIR):
            inputs, normed, inv_std, coeff = saved[layer][b]
            scaled = upstream[b].astype(f32) * gain[layer : layer + 1]
            grad_sum = inv_std * (
                scaled
                - jnp.mean(scaled, axis=1, keepdims=True)
                - normed * jnp.mean(scaled * normed, axis=1, keepdims=True)
            )
            low = grad_sum.astype(bf16)
            grad_feat = dot(low, output_ref[layer], 1, 1).astype(bf16)
            local.append(grad_sum + dot(grad_feat, coeff))
            lows.append(low)
            grad_feats.append(grad_feat)
        linear = dot(compress_ref[layer], jnp.concatenate(lows, axis=1), 0, 0)
        basis_twice = jnp.concatenate([basis_ref[layer], basis_ref[layer]], axis=1)
        for b in range(PAIR):
            grad_coeff = dot(grad_feats[b], saved[layer][b][0], 0, 0)
            high = grad_coeff.astype(bf16)
            rest = (grad_coeff - high.astype(f32)).astype(bf16)
            basis_part = dot(basis_twice, jnp.concatenate([high, rest], axis=0))
            upstream[b] = (local[b] + linear[:, b * D : (b + 1) * D] + basis_part).astype(bf16)
    shape = (DP * PAIR * CAPACITY, PAIR * SLOT_DEV)
    row = iota(shape, 0)
    row_key = row // (PAIR * CAPACITY) * CAPACITY + row % CAPACITY + row // CAPACITY % PAIR * 1024
    sample_key = iota((1, PAIR * SLOT_DEV), 1) // SLOT_DEV * 1024
    targets = []
    for k in range(N_SLOT):
        target = x_ref[k, 2 * pair_rows + ID_ROWS : 2 * pair_rows + ID_ROWS + 16, :]
        target = target[:1].astype(f32).astype(jnp.int32)
        targets.append(target)
        column_key = jnp.concatenate([target] * PAIR, axis=1) + sample_key
        placing = jnp.where(row_key == column_key, 1.0, 0.0).astype(bf16)
        rows = slice(k * SLOT_DEV, (k + 1) * SLOT_DEV)
        values = jnp.concatenate([u[rows] for u in upstream], axis=0)
        out_ref[:, k] = dot(placing, values).astype(bf16).reshape(DP, PAIR * CAPACITY, D)
    shape = (DP * 8, SLOTS)
    row = iota(shape, 0)
    row_key = row // 8 * CAPACITY + row % 8 * 1024
    column_key = jnp.concatenate([targets[k] + k * 1024 for k in range(N_SLOT)], axis=1)
    unpacked = jnp.concatenate(
        [x_ref[k, 2 * pair_rows : 2 * pair_rows + ID_ROWS, :] for k in range(N_SLOT)], axis=1
    )
    unpacked = jnp.concatenate([unpacked] * CAPACITY, axis=0)
    rank_lane = iota((1, D), 1) // 32
    ids = jnp.zeros((DP * 8, D), f32)
    for rank in range(CAPACITY):
        placing = jnp.where(row_key + rank == column_key, 1.0, 0.0).astype(bf16)
        ids = ids + jnp.where(rank_lane == rank, dot(placing, unpacked, 1, 1), 0.0)
    out_ref[:, N_SLOT] = ids.astype(bf16).reshape(DP, 8, D)


def run_layers(here, *args):
    return pl.pallas_call(
        layers_kernel,
        out_shape=jax.ShapeDtypeStruct((DP, N_SLOT + 1, 8, D), bf16),
        in_specs=[SMEM_SPEC] + [VMEM_SPEC] * len(args),
        out_specs=VMEM_SPEC,
        scratch_shapes=[pltpu.VMEM((N_SLOT, MSG_ROWS, D), bf16)],
        compiler_params=pltpu.CompilerParams(vmem_limit_bytes=20 << 20),
        cost_estimate=pl.CostEstimate(flops=2_000_000_000, bytes_accessed=4 << 20, transcendentals=4096),
        name="layers",
    )(here, *args)


def prepare_bags(got_ref, wide_ref, grads_ref, high_ref, low_ref):
    bags = PAIR * DP
    shape = (DP * 8, N_SLOT * bags)
    row = iota(shape, 0)
    lane = iota(shape, 1)
    pick = (row // 8 == lane % DP) & (row % 8 == lane // bags)
    ids = dot(
        got_ref[:, N_SLOT].reshape(DP * 8, D), jnp.where(pick, 1.0, 0.0).astype(bf16), 0, 0
    )
    first_sample = iota((1, bags), 1) < DP
    for k in range(N_SLOT):
        wide_ref[...] = got_ref[:, k].astype(f32).reshape(DP * 8, D)
        for rank in range(CAPACITY):
            cap = k * CAPACITY + rank
            both = ids[rank * 32 : (rank + 1) * 32, k * bags : (k + 1) * bags]
            own = jnp.where(first_sample, both[:16], both[16:])
            high, low = own[:8], own[8:]
            alive = jnp.where(high >= DEAD, high - DEAD, high)[:1]
            table = jnp.where(jnp.max(alive, axis=1, keepdims=True) >= 16, 1.0, 0.0)
            half = cap % 2
            lanes = slice(half * bags, (half + 1) * bags)
            high_ref[cap // 2, :, lanes] = high - 16.0 * table
            low_ref[cap // 2, :, lanes] = low
            values = jnp.concatenate(
                [wide_ref[pl.ds(b * CAPACITY + rank, DP, stride=8), :] for b in range(PAIR)], axis=0
            )
            rows = slice(half * bags, (half + 1) * bags)
            grads_ref[cap // 2, rows, :D] = (values * (1.0 - table)).astype(bf16)
            grads_ref[cap // 2, rows, D:] = (values * table).astype(bf16)


def add_rows(blocks_ref, out_ref, grads_ref, high_ref, low_ref):
    lanes = 2 * PAIR * DP
    half = ROW_BLOCK // 2
    rows_of = iota((half, lanes), 0).astype(f32).astype(bf16)
    one = jnp.ones((), bf16)
    zero = jnp.zeros((), bf16)

    def block(index, carry):
        want = blocks_ref[index].astype(f32)
        for part in range(2):
            total = jnp.zeros((half, 2 * D), f32)
            for p in range(N_SLOT * CAPACITY // 2):
                match = jnp.where(high_ref[p] == want, low_ref[p] - float(part * half), -1.0)
                count = jnp.zeros((half, lanes), bf16)
                for j in range(BAG):
                    wanted = jnp.broadcast_to(match[j : j + 1], (16, lanes)).astype(bf16)
                    wanted = jnp.broadcast_to(wanted[None], (half // 16, 16, lanes)).reshape(half, lanes)
                    count = count + jnp.where(rows_of == wanted, one, zero)
                total = total + dot(count, grads_ref[p])
            rows = slice(part * half, (part + 1) * half)
            out_ref[index // 2, index % 2, 0, rows] = total[:, :D].astype(bf16)
            out_ref[index // 2, index % 2, 1, rows] = total[:, D:].astype(bf16)
        return carry

    lax.fori_loop(0, 4, block, 0)


def first_bags_kernel(blocks_ref, got_ref, out_ref, grads_ref, high_ref, low_ref, wide_ref):
    prepare_bags(got_ref, wide_ref, grads_ref, high_ref, low_ref)
    add_rows(blocks_ref, out_ref, grads_ref, high_ref, low_ref)


def later_bags_kernel(blocks_ref, grads_ref, high_ref, low_ref, out_ref):
    add_rows(blocks_ref, out_ref, grads_ref, high_ref, low_ref)


BAGS_COST = pl.CostEstimate(flops=200_000_000, bytes_accessed=1 << 20, transcendentals=0)
ADD_COST = pl.CostEstimate(flops=1_000_000, bytes_accessed=1 << 20, transcendentals=0)
CHUNK = (TABLE_DEV, ROW_BLOCK, D)


def run_first_bags(blocks, got):
    pairs = N_SLOT * CAPACITY // 2
    lanes = 2 * PAIR * DP
    return pl.pallas_call(
        first_bags_kernel,
        out_shape=(
            jax.ShapeDtypeStruct((2, 2, *CHUNK), bf16),
            jax.ShapeDtypeStruct((pairs, lanes, 2 * D), bf16),
            jax.ShapeDtypeStruct((pairs, BAG, lanes), f32),
            jax.ShapeDtypeStruct((pairs, BAG, lanes), f32),
        ),
        in_specs=[SMEM_SPEC, VMEM_SPEC],
        out_specs=(VMEM_SPEC,) * 4,
        scratch_shapes=[pltpu.VMEM((DP * 8, D), f32)],
        compiler_params=pltpu.CompilerParams(vmem_limit_bytes=24 << 20),
        cost_estimate=BAGS_COST,
        name="first_bags",
    )(blocks, got)


def run_later_bags(blocks, prepared, name):
    return pl.pallas_call(
        later_bags_kernel,
        out_shape=jax.ShapeDtypeStruct((2, 2, *CHUNK), bf16),
        in_specs=[SMEM_SPEC] + [VMEM_SPEC] * 3,
        out_specs=VMEM_SPEC,
        compiler_params=pltpu.CompilerParams(vmem_limit_bytes=24 << 20),
        cost_estimate=BAGS_COST,
        name=name,
    )(blocks, *prepared)


def wide_sum(*refs):
    total = refs[0][...].astype(f32)
    for ref in refs[1:]:
        total = total + ref[...].astype(f32)
    return total


def add_parts_kernel(kept_ref, got_ref, own_ref, sent_ref):
    own_ref[...] = wide_sum(kept_ref.at[0], got_ref.at[0]).astype(bf16)
    sent_ref[...] = wide_sum(kept_ref.at[1], got_ref.at[1]).astype(bf16)


def sum_a_kernel(own_ref, got_ref, far_ref, after_ref):
    far_ref[...] = wide_sum(own_ref.at[0], got_ref.at[0]).astype(bf16)
    after_ref[...] = wide_sum(own_ref.at[1], got_ref.at[1]).astype(bf16)


def sum_b_kernel(own_ref, got_ref, kept_ref, before_ref):
    kept_ref[...] = wide_sum(own_ref.at[0], got_ref.at[0])
    before_ref[...] = wide_sum(own_ref.at[1], got_ref.at[1]).astype(bf16)


def final_kernel(kept_ref, far_ref, before_ref, after_ref, out_ref):
    out_ref[...] = wide_sum(kept_ref, far_ref, before_ref, after_ref)


def small_call(kernel, name, shapes, *args):
    outs = tuple(jax.ShapeDtypeStruct(shape, dtype) for shape, dtype in shapes)
    return pl.pallas_call(
        kernel,
        out_shape=outs,
        in_specs=[VMEM_SPEC] * len(args),
        out_specs=(VMEM_SPEC,) * len(outs),
        compiler_params=pltpu.CompilerParams(vmem_limit_bytes=8 << 20),
        cost_estimate=ADD_COST,
        name=name,
    )(*args)


def per_device(
    pooled,
    cotangent,
    compress_weight,
    fm_basis,
    fm_output,
    norm_gain,
    bag_ids,
    bag_lengths,
    slot_table,
    table_home,
):
    here = lax.axis_index("slot").astype(jnp.int32)
    at_slot = here.reshape(1)
    up_moves, far_moves, down_moves = (
        [(i, (i + step) % N_SLOT) for i in range(N_SLOT)] for step in (1, 2, 3)
    )
    own, to_after, to_far, to_before = make_messages(
        at_slot,
        pooled.reshape(N_SLOT, POOLED_ROWS, D),
        cotangent.reshape(N_SLOT, POOLED_ROWS, D),
        jnp.transpose(bag_ids, (0, 2, 1)),
        bag_lengths.reshape(-1, 1, SLOT_DEV),
        slot_table.reshape(1, SLOT_DEV),
        table_home.reshape(1, -1),
    )
    from_far = lax.ppermute(to_far, "slot", far_moves)
    from_before = lax.ppermute(to_after, "slot", up_moves)
    from_after = lax.ppermute(to_before, "slot", down_moves)
    sent = run_layers(
        at_slot, own, from_before, from_far, from_after, compress_weight, fm_basis, fm_output, norm_gain
    )
    got = lax.all_to_all(sent, "dp", split_axis=0, concat_axis=0, tiled=True)
    me = lax.axis_index("grp").astype(jnp.int32)
    side = me ^ 1
    mirror = N_GRP - 1 - me
    across = side ^ 3
    far, after, before = (here + 2) % N_SLOT, (here + 1) % N_SLOT, (here + 3) % N_SLOT

    def blocks(groups, chunks):
        return jnp.stack([chunk * N_GRP + group for group in groups for chunk in chunks])

    half_a, half_b = (far, after), (here, before)
    side_moves = [(i, i ^ 1) for i in range(N_GRP)]
    mirror_moves = [(i, N_GRP - 1 - i) for i in range(N_GRP)]
    a_sent, *prepared = run_first_bags(blocks((side, across), half_a), got)
    a_got = lax.ppermute(a_sent, "grp", side_moves)
    b_sent = run_later_bags(blocks((mirror, across), half_b), prepared, "b_sent")
    b_got = lax.ppermute(b_sent, "grp", mirror_moves)
    a_kept = run_later_bags(blocks((me, mirror), half_a), prepared, "a_kept")
    part = ((2, *CHUNK), bf16)
    a_own, a_next = small_call(add_parts_kernel, "add_a", (part, part), a_kept, a_got)
    a_last = lax.ppermute(a_next, "grp", mirror_moves)
    b_blocks, a_own = lax.optimization_barrier((blocks((me, side), half_b), a_own))
    b_kept = run_later_bags(b_blocks, prepared, "b_kept")
    b_own, b_next = small_call(add_parts_kernel, "add_b", (part, part), b_kept, b_got)
    b_last = lax.ppermute(b_next, "grp", side_moves)
    chunk = (CHUNK, bf16)
    to_far, to_after = small_call(sum_a_kernel, "sum_a", (chunk, chunk), a_own, a_last)
    from_far = lax.ppermute(to_far, "slot", far_moves)
    from_before = lax.ppermute(to_after, "slot", up_moves)
    kept, to_before = small_call(sum_b_kernel, "sum_b", ((CHUNK, f32), chunk), b_own, b_last)
    from_after = lax.ppermute(to_before, "slot", down_moves)
    return small_call(final_kernel, "final_sum", ((CHUNK, f32),), kept, from_far, from_before, from_after)[0]


def solution(mesh):
    in_specs = (
        P(("dp", "grp"), "slot", None),
        P(("dp", "grp"), "slot", None),
        P(),
        P(),
        P(),
        P(),
        P(("dp", "grp"), "slot", None),
        P(("dp", "grp"), "slot"),
        P("slot"),
        P(),
    )
    out_specs = P("dp", ("slot", "grp"), None)
    return jax.shard_map(
        per_device, mesh=mesh, in_specs=in_specs, out_specs=out_specs, check_vma=False
    )
```

```python
import functools

import jax
import jax.numpy as jnp
from jax import lax
from jax.experimental import pallas as pl
from jax.experimental.pallas import tpu as pltpu
from jax.sharding import PartitionSpec as P

D = 128
LAYERS = 2
ROWS = 4096
TABLE_DEV = 2
BAG = 8
CAPACITY = 4
N_SLOT = 4
N_GRP = 4
DP = 64
SLOT_DEV = 128
SLOTS = 512
RANK = 32
PAIR = 2
ROW_BLOCK = 256
DEAD = 64
ID_ROWS = 32
POOLED_ROWS = PAIR * SLOT_DEV
MSG_ROWS = 2 * POOLED_ROWS + ID_ROWS + 16

norm_eps = 1e-05
f32 = jnp.float32
bf16 = jnp.bfloat16


ANY_SPEC = pl.BlockSpec(memory_space=pl.ANY)
VMEM_SPEC = pl.BlockSpec(memory_space=pltpu.VMEM)
SMEM_SPEC = pl.BlockSpec(memory_space=pltpu.SMEM)


def dot(a, b, ca=1, cb=0):
    return lax.dot_general(a, b, (((ca,), (cb,)), ((), ())), preferred_element_type=f32)


def iota(shape, dim):
    return lax.broadcasted_iota(jnp.int32, shape, dim)


def messages_kernel(
    place_ref, pooled_ref, cotangent_ref, ids_any, lengths_any, slot_ref, home_ref, *refs
):
    out_refs, (ids_ref, lengths_ref, tail_ref, sems, small_sems) = refs[:N_SLOT], refs[N_SLOT:]
    small = [
        pltpu.make_async_copy(ids_any, ids_ref, small_sems.at[0]),
        pltpu.make_async_copy(lengths_any, lengths_ref, small_sems.at[1]),
    ]
    for copy in small:
        copy.start()
    copies = []
    for r in (2, 1, 3, 0):
        dest = lax.rem(place_ref[0] + r, N_SLOT)
        for part, source in enumerate((pooled_ref, cotangent_ref)):
            rows = pl.ds(part * POOLED_ROWS, POOLED_ROWS)
            copies.append(pltpu.make_async_copy(source.at[dest], out_refs[r].at[rows], sems.at[r, part]))
            copies[-1].start()
    slots = slot_ref[...]
    hot = jnp.where(iota((SLOT_DEV, SLOT_DEV), 0) == slots, 1.0, 0.0).astype(bf16)
    homes = jnp.broadcast_to(home_ref[...].astype(f32), (8, SLOT_DEV)).astype(bf16)
    across = dot(homes, hot)[:1].astype(jnp.int32)
    down = dot(hot, homes, 0, 1)[:, :1].astype(jnp.int32)
    earlier = iota((SLOT_DEV, SLOT_DEV), 0) < iota((SLOT_DEV, SLOT_DEV), 1)
    same = (down // TABLE_DEV == across // TABLE_DEV) & earlier
    rank = jnp.sum(jnp.where(same, 1.0, 0.0), axis=0, keepdims=True)
    target = (across // TABLE_DEV * CAPACITY).astype(f32) + rank
    table = across % TABLE_DEV * 16
    marks = jnp.broadcast_to(target, (16, SLOT_DEV)).astype(bf16)
    entry = iota((BAG, SLOT_DEV), 0)
    for copy in small:
        copy.wait()
    for r, out_ref in enumerate(out_refs):
        dest = lax.rem(place_ref[0] + r, N_SLOT)
        parts = []
        for b in range(PAIR):
            ids = ids_ref[dest * PAIR + b]
            live = entry < lengths_ref[pl.ds(dest * PAIR + b, 1), :]
            parts.append((jnp.where(live, ids // ROW_BLOCK, DEAD) + table).astype(f32))
            parts.append((ids % ROW_BLOCK).astype(f32))
        tail_ref[r, :ID_ROWS] = jnp.concatenate(parts, axis=0).astype(bf16)
        tail_ref[r, ID_ROWS:] = marks
        rows = pl.ds(2 * POOLED_ROWS, ID_ROWS + 16)
        copies.append(pltpu.make_async_copy(tail_ref.at[r], out_ref.at[rows], sems.at[r, 2]))
        copies[-1].start()
    for copy in copies:
        copy.wait()


def make_messages(place, *args):
    message = jax.ShapeDtypeStruct((MSG_ROWS, D), bf16)
    return pl.pallas_call(
        messages_kernel,
        out_shape=(message,) * N_SLOT,
        in_specs=[SMEM_SPEC] + [ANY_SPEC] * 4 + [VMEM_SPEC] * 2,
        out_specs=(ANY_SPEC,) * N_SLOT,
        scratch_shapes=[
            pltpu.VMEM((N_SLOT * PAIR, BAG, SLOT_DEV), jnp.int32),
            pltpu.VMEM((N_SLOT * PAIR, SLOT_DEV), jnp.int32),
            pltpu.VMEM((N_SLOT, ID_ROWS + 16, SLOT_DEV), bf16),
            pltpu.SemaphoreType.DMA((N_SLOT, 3)),
            pltpu.SemaphoreType.DMA((2,)),
        ],
        compiler_params=pltpu.CompilerParams(vmem_limit_bytes=56 << 20),
        cost_estimate=pl.CostEstimate(flops=1_000_000, bytes_accessed=2 << 20, transcendentals=0),
        name="messages",
    )(place, *args)


def layers_kernel(
    place_ref, own_ref, before_ref, far_ref, after_ref, compress_any, basis_ref, output_ref, gain_ref,
    out_ref, x_ref, compress_ref, sems
):
    inputs = []
    for r, ref in enumerate((own_ref, after_ref, far_ref, before_ref)):
        index = lax.rem(place_ref[0] + r, N_SLOT)
        inputs.append(pltpu.make_async_copy(ref, x_ref.at[index], sems.at[LAYERS + r]))
        inputs[-1].start()
    fetches = [
        pltpu.make_async_copy(compress_any.at[k], compress_ref.at[k], sems.at[k]) for k in range(LAYERS)
    ]
    for fetch in fetches:
        fetch.start()
    for copy in inputs:
        copy.wait()
    gain = gain_ref[...]
    pair_rows = POOLED_ROWS
    current = []
    upstream = []
    for b in range(PAIR):
        rows = slice(b * SLOT_DEV, (b + 1) * SLOT_DEV)
        current.append(jnp.concatenate([x_ref[k, rows, :] for k in range(N_SLOT)], axis=0))
        rows = slice(pair_rows + b * SLOT_DEV, pair_rows + (b + 1) * SLOT_DEV)
        upstream.append(jnp.concatenate([x_ref[k, rows, :] for k in range(N_SLOT)], axis=0))
    saved = []
    for layer in range(LAYERS):
        wide = jnp.concatenate(current, axis=1)
        coefficient = dot(basis_ref[layer], wide, 0, 0).astype(bf16)
        fetches[layer].wait()
        mixed = dot(compress_ref[layer], wide)
        following = []
        entry = []
        for b in range(PAIR):
            lanes = slice(b * D, (b + 1) * D)
            coeff = coefficient[:, lanes]
            feature = dot(current[b], coeff, 1, 1).astype(bf16)
            total = current[b].astype(f32) + dot(feature, output_ref[layer]) + mixed[:, lanes]
            mean = jnp.mean(total, axis=1, keepdims=True)
            centered = total - mean
            variance = jnp.mean(centered * centered, axis=1, keepdims=True)
            inv_std = lax.rsqrt(variance + norm_eps)
            normed = centered * inv_std
            entry.append((current[b], normed, inv_std, coeff))
            following.append((normed * gain[layer : layer + 1]).astype(bf16))
        saved.append(entry)
        current = following
    for layer in reversed(range(LAYERS)):
        lows = []
        local = []
        grad_feats = []
        for b in range(PAIR):
            inputs, normed, inv_std, coeff = saved[layer][b]
            scaled = upstream[b].astype(f32) * gain[layer : layer + 1]
            grad_sum = inv_std * (
                scaled
                - jnp.mean(scaled, axis=1, keepdims=True)
                - normed * jnp.mean(scaled * normed, axis=1, keepdims=True)
            )
            low = grad_sum.astype(bf16)
            grad_feat = dot(low, output_ref[layer], 1, 1).astype(bf16)
            local.append(grad_sum + dot(grad_feat, coeff))
            lows.append(low)
            grad_feats.append(grad_feat)
        linear = dot(compress_ref[layer], jnp.concatenate(lows, axis=1), 0, 0)
        basis_twice = jnp.concatenate([basis_ref[layer], basis_ref[layer]], axis=1)
        for b in range(PAIR):
            grad_coeff = dot(grad_feats[b], saved[layer][b][0], 0, 0)
            high = grad_coeff.astype(bf16)
            rest = (grad_coeff - high.astype(f32)).astype(bf16)
            basis_part = dot(basis_twice, jnp.concatenate([high, rest], axis=0))
            upstream[b] = (local[b] + linear[:, b * D : (b + 1) * D] + basis_part).astype(bf16)
    shape = (DP * PAIR * CAPACITY, PAIR * SLOT_DEV)
    row = iota(shape, 0)
    row_key = row // (PAIR * CAPACITY) * CAPACITY + row % CAPACITY + row // CAPACITY % PAIR * 1024
    sample_key = iota((1, PAIR * SLOT_DEV), 1) // SLOT_DEV * 1024
    targets = []
    for k in range(N_SLOT):
        target = x_ref[k, 2 * pair_rows + ID_ROWS : 2 * pair_rows + ID_ROWS + 16, :]
        target = target[:1].astype(f32).astype(jnp.int32)
        targets.append(target)
        column_key = jnp.concatenate([target] * PAIR, axis=1) + sample_key
        placing = jnp.where(row_key == column_key, 1.0, 0.0).astype(bf16)
        rows = slice(k * SLOT_DEV, (k + 1) * SLOT_DEV)
        values = jnp.concatenate([u[rows] for u in upstream], axis=0)
        out_ref[:, k] = dot(placing, values).astype(bf16).reshape(DP, PAIR * CAPACITY, D)
    shape = (DP * 8, SLOTS)
    row = iota(shape, 0)
    row_key = row // 8 * CAPACITY + row % 8 * 1024
    column_key = jnp.concatenate([targets[k] + k * 1024 for k in range(N_SLOT)], axis=1)
    unpacked = jnp.concatenate(
        [x_ref[k, 2 * pair_rows : 2 * pair_rows + ID_ROWS, :] for k in range(N_SLOT)], axis=1
    )
    unpacked = jnp.concatenate([unpacked] * CAPACITY, axis=0)
    rank_lane = iota((1, D), 1) // 32
    ids = jnp.zeros((DP * 8, D), f32)
    for rank in range(CAPACITY):
        placing = jnp.where(row_key + rank == column_key, 1.0, 0.0).astype(bf16)
        ids = ids + jnp.where(rank_lane == rank, dot(placing, unpacked, 1, 1), 0.0)
    out_ref[:, N_SLOT] = ids.astype(bf16).reshape(DP, 8, D)


def run_layers(place, *args):
    return pl.pallas_call(
        layers_kernel,
        out_shape=jax.ShapeDtypeStruct((DP, N_SLOT + 1, 8, D), bf16),
        in_specs=[SMEM_SPEC] + [ANY_SPEC] * 5 + [VMEM_SPEC] * 3,
        out_specs=VMEM_SPEC,
        scratch_shapes=[
            pltpu.VMEM((N_SLOT, MSG_ROWS, D), bf16),
            pltpu.VMEM((LAYERS, SLOTS, SLOTS), bf16),
            pltpu.SemaphoreType.DMA((LAYERS + N_SLOT,)),
        ],
        compiler_params=pltpu.CompilerParams(vmem_limit_bytes=56 << 20),
        cost_estimate=pl.CostEstimate(flops=2_000_000_000, bytes_accessed=4 << 20, transcendentals=4096),
        name="layers",
    )(place, *args)


def prepare_bags(got_ref, wide_ref, grads_ref, high_ref, low_ref):
    bags = PAIR * DP
    shape = (DP * 8, N_SLOT * bags)
    row = iota(shape, 0)
    lane = iota(shape, 1)
    pick = (row // 8 == lane % DP) & (row % 8 == lane // bags)
    ids = dot(
        got_ref[:, N_SLOT].reshape(DP * 8, D), jnp.where(pick, 1.0, 0.0).astype(bf16), 0, 0
    )
    first_sample = iota((1, bags), 1) < DP
    for k in range(N_SLOT):
        wide_ref[...] = got_ref[:, k].astype(f32).reshape(DP * 8, D)
        for rank in range(CAPACITY):
            cap = k * CAPACITY + rank
            both = ids[rank * 32 : (rank + 1) * 32, k * bags : (k + 1) * bags]
            own = jnp.where(first_sample, both[:16], both[16:])
            high, low = own[:8], own[8:]
            alive = jnp.where(high >= DEAD, high - DEAD, high)[:1]
            table = jnp.where(jnp.max(alive, axis=1, keepdims=True) >= 16, 1.0, 0.0)
            half = cap % 2
            lanes = slice(half * bags, (half + 1) * bags)
            high_ref[cap // 2, :, lanes] = high - 16.0 * table
            low_ref[cap // 2, :, lanes] = low
            values = jnp.concatenate(
                [wide_ref[pl.ds(b * CAPACITY + rank, DP, stride=8), :] for b in range(PAIR)], axis=0
            )
            rows = slice(half * bags, (half + 1) * bags)
            grads_ref[cap // 2, rows, :D] = (values * (1.0 - table)).astype(bf16)
            grads_ref[cap // 2, rows, D:] = (values * table).astype(bf16)


def add_rows(ahead, place_ref, out_ref, grads_ref, high_ref, low_ref, more_ref=None):
    lanes = 2 * PAIR * DP
    half = ROW_BLOCK // 2
    rows_of = iota((half, lanes), 0).astype(f32).astype(bf16)
    one = jnp.ones((), bf16)
    zero = jnp.zeros((), bf16)

    def block(index, carry):
        chunk = lax.rem(place_ref[0] + index, N_SLOT)
        group = lax.rem(place_ref[1] + ahead, N_GRP)
        want = (chunk * N_GRP + group).astype(f32)
        for part in range(2):
            total = jnp.zeros((half, 2 * D), f32)
            for p in range(N_SLOT * CAPACITY // 2):
                match = jnp.where(high_ref[p] == want, low_ref[p] - float(part * half), -1.0)
                count = jnp.zeros((half, lanes), bf16)
                for j in range(BAG):
                    wanted = jnp.broadcast_to(match[j : j + 1], (16, lanes)).astype(bf16)
                    wanted = jnp.broadcast_to(wanted[None], (half // 16, 16, lanes)).reshape(half, lanes)
                    count = count + jnp.where(rows_of == wanted, one, zero)
                total = total + dot(count, grads_ref[p])
            rows = slice(part * half, (part + 1) * half)
            sums = [total[:, :D], total[:, D:]]
            if more_ref is not None:
                sums = [sums[t] + more_ref[index, t, rows].astype(f32) for t in range(TABLE_DEV)]
            for t in range(TABLE_DEV):
                out_ref[index, t, rows] = sums[t].astype(bf16)
        return carry

    lax.fori_loop(0, N_SLOT, block, 0)


def first_bags_kernel(ahead, place_ref, got_ref, out_ref, grads_ref, high_ref, low_ref, wide_ref):
    prepare_bags(got_ref, wide_ref, grads_ref, high_ref, low_ref)
    add_rows(ahead, place_ref, out_ref, grads_ref, high_ref, low_ref)


def later_bags_kernel(ahead, place_ref, grads_ref, high_ref, low_ref, *refs):
    add_rows(ahead, place_ref, refs[-1], grads_ref, high_ref, low_ref, *refs[:-1])


BAGS_COST = pl.CostEstimate(flops=1000, bytes_accessed=1000, transcendentals=0)
ADD_COST = pl.CostEstimate(flops=1_000_000, bytes_accessed=1 << 20, transcendentals=0)
CHUNK = (TABLE_DEV, ROW_BLOCK, D)


def run_first_bags(ahead, place, got):
    pairs = N_SLOT * CAPACITY // 2
    lanes = 2 * PAIR * DP
    return pl.pallas_call(
        functools.partial(first_bags_kernel, ahead),
        out_shape=(
            jax.ShapeDtypeStruct((N_SLOT, *CHUNK), bf16),
            jax.ShapeDtypeStruct((pairs, lanes, 2 * D), bf16),
            jax.ShapeDtypeStruct((pairs, BAG, lanes), f32),
            jax.ShapeDtypeStruct((pairs, BAG, lanes), f32),
        ),
        in_specs=[SMEM_SPEC, VMEM_SPEC],
        out_specs=(VMEM_SPEC,) * 4,
        scratch_shapes=[pltpu.VMEM((DP * 8, D), f32)],
        compiler_params=pltpu.CompilerParams(vmem_limit_bytes=24 << 20),
        cost_estimate=BAGS_COST,
        name="first_bags",
    )(place, got)


def run_later_bags(ahead, place, prepared, name, *more):
    return pl.pallas_call(
        functools.partial(later_bags_kernel, ahead),
        out_shape=jax.ShapeDtypeStruct((N_SLOT, *CHUNK), bf16),
        in_specs=[SMEM_SPEC] + [VMEM_SPEC] * (3 + len(more)),
        out_specs=VMEM_SPEC,
        compiler_params=pltpu.CompilerParams(vmem_limit_bytes=24 << 20),
        cost_estimate=BAGS_COST,
        name=name,
    )(place, *prepared, *more)


def wide_sum(*refs):
    total = refs[0][...].astype(f32)
    for ref in refs[1:]:
        total = total + ref[...].astype(f32)
    return total


def grp_sum_kernel(own_ref, a_ref, b_ref, kept_ref, after_ref, far_ref, before_ref):
    parts = (own_ref, a_ref, b_ref)
    kept_ref[...] = wide_sum(*(part.at[0] for part in parts))
    for r, ref in ((1, after_ref), (2, far_ref), (3, before_ref)):
        ref[...] = wide_sum(*(part.at[r] for part in parts)).astype(bf16)


def final_kernel(kept_ref, far_ref, before_ref, after_ref, out_ref):
    out_ref[...] = wide_sum(kept_ref, far_ref, before_ref, after_ref)


def small_call(kernel, name, shapes, *args):
    outs = tuple(jax.ShapeDtypeStruct(shape, dtype) for shape, dtype in shapes)
    return pl.pallas_call(
        kernel,
        out_shape=outs,
        in_specs=[VMEM_SPEC] * len(args),
        out_specs=(VMEM_SPEC,) * len(outs),
        compiler_params=pltpu.CompilerParams(vmem_limit_bytes=8 << 20),
        cost_estimate=ADD_COST,
        name=name,
    )(*args)


def per_device(
    pooled,
    cotangent,
    compress_weight,
    fm_basis,
    fm_output,
    norm_gain,
    bag_ids,
    bag_lengths,
    slot_table,
    table_home,
):
    place = jnp.stack([lax.axis_index("slot"), lax.axis_index("grp")]).astype(jnp.int32)
    up_moves, far_moves, down_moves = (
        [(i, (i + step) % N_SLOT) for i in range(N_SLOT)] for step in (1, 2, 3)
    )
    own, to_after, to_far, to_before = make_messages(
        place,
        pooled.reshape(N_SLOT, POOLED_ROWS, D),
        cotangent.reshape(N_SLOT, POOLED_ROWS, D),
        jnp.transpose(bag_ids, (0, 2, 1)),
        bag_lengths,
        slot_table.reshape(1, SLOT_DEV),
        table_home.reshape(1, -1),
    )
    from_far = lax.ppermute(to_far, "slot", far_moves)
    from_before = lax.ppermute(to_after, "slot", up_moves)
    from_after = lax.ppermute(to_before, "slot", down_moves)
    sent = run_layers(
        place, own, from_before, from_far, from_after, compress_weight, fm_basis, fm_output, norm_gain
    )
    got = lax.all_to_all(sent, "dp", split_axis=0, concat_axis=0, tiled=True)
    far_part, *prepared = run_first_bags(2, place, got)
    far_part = lax.ppermute(far_part, "grp", far_moves)
    next_part = run_later_bags(1, place, prepared, "next_rows")
    next_part = lax.ppermute(next_part, "grp", up_moves)
    last_part = run_later_bags(3, place, prepared, "last_rows")
    last_part = lax.ppermute(last_part, "grp", down_moves)
    own_part = run_later_bags(0, place, prepared, "own_rows", far_part)
    chunk = (CHUNK, bf16)
    kept, to_after, to_far, to_before = small_call(
        grp_sum_kernel, "grp_sum", ((CHUNK, f32), chunk, chunk, chunk), own_part, next_part, last_part
    )
    from_far = lax.ppermute(to_far, "slot", far_moves)
    from_before = lax.ppermute(to_after, "slot", up_moves)
    from_after = lax.ppermute(to_before, "slot", down_moves)
    return small_call(final_kernel, "final_sum", ((CHUNK, f32),), kept, from_far, from_before, from_after)[0]


def solution(mesh):
    in_specs = (
        P(("dp", "grp"), "slot", None),
        P(("dp", "grp"), "slot", None),
        P(),
        P(),
        P(),
        P(),
        P(("dp", "grp"), "slot", None),
        P(("dp", "grp"), "slot"),
        P("slot"),
        P(),
    )
    out_specs = P("dp", ("slot", "grp"), None)
    return jax.shard_map(
        per_device, mesh=mesh, in_specs=in_specs, out_specs=out_specs, check_vma=False
    )
```

```python
import functools

import jax
import jax.numpy as jnp
from jax import lax
from jax.experimental import pallas as pl
from jax.experimental.pallas import tpu as pltpu
from jax.sharding import PartitionSpec as P

D = 128
LAYERS = 2
ROWS = 4096
TABLE_DEV = 2
BAG = 8
CAPACITY = 4
N_SLOT = 4
N_GRP = 4
DP = 64
SLOT_DEV = 128
SLOTS = 512
RANK = 32
PAIR = 2
ROW_BLOCK = 256
DEAD = 64
ID_ROWS = 32
POOLED_ROWS = PAIR * SLOT_DEV
MSG_ROWS = 2 * POOLED_ROWS + ID_ROWS + 16

norm_eps = 1e-05
f32 = jnp.float32
bf16 = jnp.bfloat16


ANY_SPEC = pl.BlockSpec(memory_space=pl.ANY)
VMEM_SPEC = pl.BlockSpec(memory_space=pltpu.VMEM)
SMEM_SPEC = pl.BlockSpec(memory_space=pltpu.SMEM)


def dot(a, b, ca=1, cb=0):
    return lax.dot_general(a, b, (((ca,), (cb,)), ((), ())), preferred_element_type=f32)


def iota(shape, dim):
    return lax.broadcasted_iota(jnp.int32, shape, dim)


def messages_kernel(place_ref, pooled_any, cotangent_any, ids_any, lengths_any, slot_ref, home_ref, *refs):
    out_refs, (x_ref, ids_ref, lengths_ref, sems, small_sems) = refs[:N_SLOT], refs[N_SLOT:]
    small = [
        pltpu.make_async_copy(ids_any, ids_ref, small_sems.at[0]),
        pltpu.make_async_copy(lengths_any, lengths_ref, small_sems.at[1]),
    ]
    for copy in small:
        copy.start()
    fetches = []
    for part, source in enumerate((pooled_any, cotangent_any)):
        rows = pl.ds(part * POOLED_ROWS, POOLED_ROWS)
        for r in range(N_SLOT):
            dest = lax.rem(place_ref[0] + r, N_SLOT)
            fetches.append(pltpu.make_async_copy(source.at[dest], x_ref.at[r, rows], sems.at[part, r]))
            fetches[-1].start()
    slots = slot_ref[...]
    hot = jnp.where(iota((SLOT_DEV, SLOT_DEV), 0) == slots, 1.0, 0.0).astype(bf16)
    homes = jnp.broadcast_to(home_ref[...].astype(f32), (8, SLOT_DEV)).astype(bf16)
    across = dot(homes, hot)[:1].astype(jnp.int32)
    down = dot(hot, homes, 0, 1)[:, :1].astype(jnp.int32)
    earlier = iota((SLOT_DEV, SLOT_DEV), 0) < iota((SLOT_DEV, SLOT_DEV), 1)
    same = (down // TABLE_DEV == across // TABLE_DEV) & earlier
    rank = jnp.sum(jnp.where(same, 1.0, 0.0), axis=0, keepdims=True)
    target = (across // TABLE_DEV * CAPACITY).astype(f32) + rank
    table = across % TABLE_DEV * 16
    marks = jnp.broadcast_to(target, (16, SLOT_DEV)).astype(bf16)
    entry = iota((BAG, SLOT_DEV), 0)
    for copy in small:
        copy.wait()
    for r in range(N_SLOT):
        dest = lax.rem(place_ref[0] + r, N_SLOT)
        parts = []
        for b in range(PAIR):
            ids = ids_ref[dest * PAIR + b]
            live = entry < lengths_ref[pl.ds(dest * PAIR + b, 1), :]
            parts.append((jnp.where(live, ids // ROW_BLOCK, DEAD) + table).astype(f32))
            parts.append((ids % ROW_BLOCK).astype(f32))
        x_ref[r, 2 * POOLED_ROWS : 2 * POOLED_ROWS + ID_ROWS] = jnp.concatenate(parts, axis=0).astype(bf16)
        x_ref[r, 2 * POOLED_ROWS + ID_ROWS :] = marks
    for copy in fetches:
        copy.wait()
    stores = [pltpu.make_async_copy(x_ref.at[r], out_refs[r], sems.at[2, r]) for r in range(N_SLOT)]
    for copy in stores:
        copy.start()
    for copy in stores:
        copy.wait()


def make_messages(place, *args):
    message = jax.ShapeDtypeStruct((MSG_ROWS, D), bf16)
    return pl.pallas_call(
        messages_kernel,
        out_shape=(message,) * N_SLOT,
        in_specs=[SMEM_SPEC] + [ANY_SPEC] * 4 + [VMEM_SPEC] * 2,
        out_specs=(ANY_SPEC,) * N_SLOT,
        scratch_shapes=[
            pltpu.VMEM((N_SLOT, MSG_ROWS, D), bf16),
            pltpu.VMEM((N_SLOT * PAIR, BAG, SLOT_DEV), jnp.int32),
            pltpu.VMEM((N_SLOT * PAIR, SLOT_DEV), jnp.int32),
            pltpu.SemaphoreType.DMA((3, N_SLOT)),
            pltpu.SemaphoreType.DMA((2,)),
        ],
        compiler_params=pltpu.CompilerParams(vmem_limit_bytes=56 << 20),
        cost_estimate=pl.CostEstimate(flops=1_000_000, bytes_accessed=2 << 20, transcendentals=0),
        name="messages",
    )(place, *args)


def layers_kernel(
    here_ref, own_ref, before_ref, far_ref, after_ref, compress_ref, basis_ref, output_ref, gain_ref, out_ref, x_ref
):
    for r, ref in enumerate((own_ref, after_ref, far_ref, before_ref)):
        x_ref[lax.rem(here_ref[0] + r, N_SLOT)] = ref[...]
    gain = gain_ref[...]
    pair_rows = POOLED_ROWS
    current = []
    upstream = []
    for b in range(PAIR):
        rows = slice(b * SLOT_DEV, (b + 1) * SLOT_DEV)
        current.append(jnp.concatenate([x_ref[k, rows, :] for k in range(N_SLOT)], axis=0))
        rows = slice(pair_rows + b * SLOT_DEV, pair_rows + (b + 1) * SLOT_DEV)
        upstream.append(jnp.concatenate([x_ref[k, rows, :] for k in range(N_SLOT)], axis=0))
    saved = []
    for layer in range(LAYERS):
        wide = jnp.concatenate(current, axis=1)
        coefficient = dot(basis_ref[layer], wide, 0, 0).astype(bf16)
        mixed = dot(compress_ref[layer], wide)
        following = []
        entry = []
        for b in range(PAIR):
            lanes = slice(b * D, (b + 1) * D)
            coeff = coefficient[:, lanes]
            feature = dot(current[b], coeff, 1, 1).astype(bf16)
            total = current[b].astype(f32) + dot(feature, output_ref[layer]) + mixed[:, lanes]
            mean = jnp.mean(total, axis=1, keepdims=True)
            centered = total - mean
            variance = jnp.mean(centered * centered, axis=1, keepdims=True)
            inv_std = lax.rsqrt(variance + norm_eps)
            normed = centered * inv_std
            entry.append((current[b], normed, inv_std, coeff))
            following.append((normed * gain[layer : layer + 1]).astype(bf16))
        saved.append(entry)
        current = following
    for layer in reversed(range(LAYERS)):
        lows = []
        local = []
        grad_feats = []
        for b in range(PAIR):
            inputs, normed, inv_std, coeff = saved[layer][b]
            scaled = upstream[b].astype(f32) * gain[layer : layer + 1]
            grad_sum = inv_std * (
                scaled
                - jnp.mean(scaled, axis=1, keepdims=True)
                - normed * jnp.mean(scaled * normed, axis=1, keepdims=True)
            )
            low = grad_sum.astype(bf16)
            grad_feat = dot(low, output_ref[layer], 1, 1).astype(bf16)
            local.append(grad_sum + dot(grad_feat, coeff))
            lows.append(low)
            grad_feats.append(grad_feat)
        linear = dot(compress_ref[layer], jnp.concatenate(lows, axis=1), 0, 0)
        basis_twice = jnp.concatenate([basis_ref[layer], basis_ref[layer]], axis=1)
        for b in range(PAIR):
            grad_coeff = dot(grad_feats[b], saved[layer][b][0], 0, 0)
            high = grad_coeff.astype(bf16)
            rest = (grad_coeff - high.astype(f32)).astype(bf16)
            basis_part = dot(basis_twice, jnp.concatenate([high, rest], axis=0))
            upstream[b] = (local[b] + linear[:, b * D : (b + 1) * D] + basis_part).astype(bf16)
    shape = (DP * PAIR * CAPACITY, PAIR * SLOT_DEV)
    row = iota(shape, 0)
    row_key = row // (PAIR * CAPACITY) * CAPACITY + row % CAPACITY + row // CAPACITY % PAIR * 1024
    sample_key = iota((1, PAIR * SLOT_DEV), 1) // SLOT_DEV * 1024
    targets = []
    for k in range(N_SLOT):
        target = x_ref[k, 2 * pair_rows + ID_ROWS : 2 * pair_rows + ID_ROWS + 16, :]
        target = target[:1].astype(f32).astype(jnp.int32)
        targets.append(target)
        column_key = jnp.concatenate([target] * PAIR, axis=1) + sample_key
        placing = jnp.where(row_key == column_key, 1.0, 0.0).astype(bf16)
        rows = slice(k * SLOT_DEV, (k + 1) * SLOT_DEV)
        values = jnp.concatenate([u[rows] for u in upstream], axis=0)
        out_ref[:, k] = dot(placing, values).astype(bf16).reshape(DP, PAIR * CAPACITY, D)
    shape = (DP * 8, SLOTS)
    row = iota(shape, 0)
    row_key = row // 8 * CAPACITY + row % 8 * 1024
    column_key = jnp.concatenate([targets[k] + k * 1024 for k in range(N_SLOT)], axis=1)
    unpacked = jnp.concatenate(
        [x_ref[k, 2 * pair_rows : 2 * pair_rows + ID_ROWS, :] for k in range(N_SLOT)], axis=1
    )
    unpacked = jnp.concatenate([unpacked] * CAPACITY, axis=0)
    rank_lane = iota((1, D), 1) // 32
    ids = jnp.zeros((DP * 8, D), f32)
    for rank in range(CAPACITY):
        placing = jnp.where(row_key + rank == column_key, 1.0, 0.0).astype(bf16)
        ids = ids + jnp.where(rank_lane == rank, dot(placing, unpacked, 1, 1), 0.0)
    out_ref[:, N_SLOT] = ids.astype(bf16).reshape(DP, 8, D)


def fetch_kernel(source_any, out_ref, sem):
    copy = pltpu.make_async_copy(source_any, out_ref, sem)
    copy.start()
    copy.wait()


def fetch(source):
    return pl.pallas_call(
        fetch_kernel,
        out_shape=jax.ShapeDtypeStruct(source.shape, source.dtype),
        in_specs=[ANY_SPEC],
        out_specs=VMEM_SPEC,
        scratch_shapes=[pltpu.SemaphoreType.DMA],
        compiler_params=pltpu.CompilerParams(vmem_limit_bytes=8 << 20),
        cost_estimate=pl.CostEstimate(flops=0, bytes_accessed=2 << 20, transcendentals=0),
        name="fetch_weights",
    )(source)


def run_layers(here, *args):
    return pl.pallas_call(
        layers_kernel,
        out_shape=jax.ShapeDtypeStruct((DP, N_SLOT + 1, 8, D), bf16),
        in_specs=[SMEM_SPEC] + [VMEM_SPEC] * len(args),
        out_specs=VMEM_SPEC,
        scratch_shapes=[pltpu.VMEM((N_SLOT, MSG_ROWS, D), bf16)],
        compiler_params=pltpu.CompilerParams(vmem_limit_bytes=20 << 20),
        cost_estimate=pl.CostEstimate(flops=2_000_000_000, bytes_accessed=4 << 20, transcendentals=4096),
        name="layers",
    )(here, *args)


def prepare_bags(got_ref, wide_ref, grads_ref, high_ref, low_ref):
    bags = PAIR * DP
    shape = (DP * 8, N_SLOT * bags)
    row = iota(shape, 0)
    lane = iota(shape, 1)
    pick = (row // 8 == lane % DP) & (row % 8 == lane // bags)
    ids = dot(
        got_ref[:, N_SLOT].reshape(DP * 8, D), jnp.where(pick, 1.0, 0.0).astype(bf16), 0, 0
    )
    first_sample = iota((1, bags), 1) < DP
    for k in range(N_SLOT):
        wide_ref[...] = got_ref[:, k].astype(f32).reshape(DP * 8, D)
        for rank in range(CAPACITY):
            cap = k * CAPACITY + rank
            both = ids[rank * 32 : (rank + 1) * 32, k * bags : (k + 1) * bags]
            own = jnp.where(first_sample, both[:16], both[16:])
            high, low = own[:8], own[8:]
            alive = jnp.where(high >= DEAD, high - DEAD, high)[:1]
            table = jnp.where(jnp.max(alive, axis=1, keepdims=True) >= 16, 1.0, 0.0)
            half = cap % 2
            lanes = slice(half * bags, (half + 1) * bags)
            high_ref[cap // 2, :, lanes] = high - 16.0 * table
            low_ref[cap // 2, :, lanes] = low
            values = jnp.concatenate(
                [wide_ref[pl.ds(b * CAPACITY + rank, DP, stride=8), :] for b in range(PAIR)], axis=0
            )
            rows = slice(half * bags, (half + 1) * bags)
            grads_ref[cap // 2, rows, :D] = (values * (1.0 - table)).astype(bf16)
            grads_ref[cap // 2, rows, D:] = (values * table).astype(bf16)


def add_rows(blocks_ref, out_ref, grads_ref, high_ref, low_ref):
    lanes = 2 * PAIR * DP
    rows_of = iota((ROW_BLOCK, lanes), 0).astype(f32).astype(bf16)
    zero = jnp.zeros((), bf16)

    def spread(row):
        row = jnp.broadcast_to(row, (16, lanes)).astype(bf16)
        return jnp.broadcast_to(row[None], (ROW_BLOCK // 16, 16, lanes)).reshape(ROW_BLOCK, lanes)

    def block(index, carry):
        first = blocks_ref[2 * index].astype(f32)
        second = blocks_ref[2 * index + 1].astype(f32)
        totals = [jnp.zeros((ROW_BLOCK, 2 * D), f32)] * 2
        for p in range(N_SLOT * CAPACITY // 2):
            high = high_ref[p]
            low = low_ref[p]
            weight = jnp.where(high == first, 1.0, jnp.where(high == second, 16.0, 0.0))
            packed = jnp.zeros((ROW_BLOCK, lanes), bf16)
            for j in range(BAG):
                hit = rows_of == spread(low[j : j + 1])
                packed = packed + jnp.where(hit, spread(weight[j : j + 1]), zero)
            upper = ((packed - 7.5) + 3072.0) - 3072.0
            totals = [totals[0] + dot(packed - upper, grads_ref[p]), totals[1] + dot(upper, grads_ref[p])]
        for c, scale in ((0, 1.0), (1, 0.0625)):
            total = totals[c] * scale
            out_ref[index, c, 0] = total[:, :D].astype(bf16)
            out_ref[index, c, 1] = total[:, D:].astype(bf16)
        return carry

    lax.fori_loop(0, 2, block, 0)


def first_bags_kernel(blocks_ref, got_ref, out_ref, grads_ref, high_ref, low_ref, wide_ref):
    prepare_bags(got_ref, wide_ref, grads_ref, high_ref, low_ref)
    add_rows(blocks_ref, out_ref, grads_ref, high_ref, low_ref)


def later_bags_kernel(blocks_ref, grads_ref, high_ref, low_ref, out_ref):
    add_rows(blocks_ref, out_ref, grads_ref, high_ref, low_ref)


BAGS_COST = pl.CostEstimate(flops=200_000_000, bytes_accessed=1 << 20, transcendentals=0)
ADD_COST = pl.CostEstimate(flops=1_000_000, bytes_accessed=1 << 20, transcendentals=0)
CHUNK = (TABLE_DEV, ROW_BLOCK, D)


def run_first_bags(blocks, got):
    pairs = N_SLOT * CAPACITY // 2
    lanes = 2 * PAIR * DP
    return pl.pallas_call(
        first_bags_kernel,
        out_shape=(
            jax.ShapeDtypeStruct((2, 2, *CHUNK), bf16),
            jax.ShapeDtypeStruct((pairs, lanes, 2 * D), bf16),
            jax.ShapeDtypeStruct((pairs, BAG, lanes), f32),
            jax.ShapeDtypeStruct((pairs, BAG, lanes), f32),
        ),
        in_specs=[SMEM_SPEC, VMEM_SPEC],
        out_specs=(VMEM_SPEC,) * 4,
        scratch_shapes=[pltpu.VMEM((DP * 8, D), f32)],
        compiler_params=pltpu.CompilerParams(vmem_limit_bytes=24 << 20),
        cost_estimate=BAGS_COST,
        name="first_bags",
    )(blocks, got)


def run_later_bags(blocks, prepared, name):
    return pl.pallas_call(
        later_bags_kernel,
        out_shape=jax.ShapeDtypeStruct((2, 2, *CHUNK), bf16),
        in_specs=[SMEM_SPEC] + [VMEM_SPEC] * 3,
        out_specs=VMEM_SPEC,
        compiler_params=pltpu.CompilerParams(vmem_limit_bytes=24 << 20),
        cost_estimate=BAGS_COST,
        name=name,
    )(blocks, *prepared)


def wide_sum(*refs):
    total = refs[0][...].astype(f32)
    for ref in refs[1:]:
        total = total + ref[...].astype(f32)
    return total


def add_parts_kernel(kept_ref, got_ref, own_ref, sent_ref):
    own_ref[...] = wide_sum(kept_ref.at[0], got_ref.at[0]).astype(bf16)
    sent_ref[...] = wide_sum(kept_ref.at[1], got_ref.at[1]).astype(bf16)


def sum_a_kernel(own_ref, got_ref, far_ref, after_ref):
    far_ref[...] = wide_sum(own_ref.at[0], got_ref.at[0]).astype(bf16)
    after_ref[...] = wide_sum(own_ref.at[1], got_ref.at[1]).astype(bf16)


def sum_b_kernel(own_ref, got_ref, kept_ref, before_ref):
    kept_ref[...] = wide_sum(own_ref.at[0], got_ref.at[0])
    before_ref[...] = wide_sum(own_ref.at[1], got_ref.at[1]).astype(bf16)


def final_kernel(kept_ref, far_ref, before_ref, after_ref, out_ref):
    out_ref[...] = wide_sum(kept_ref, far_ref, before_ref, after_ref)


def small_call(kernel, name, shapes, *args):
    outs = tuple(jax.ShapeDtypeStruct(shape, dtype) for shape, dtype in shapes)
    return pl.pallas_call(
        kernel,
        out_shape=outs,
        in_specs=[VMEM_SPEC] * len(args),
        out_specs=(VMEM_SPEC,) * len(outs),
        compiler_params=pltpu.CompilerParams(vmem_limit_bytes=8 << 20),
        cost_estimate=ADD_COST,
        name=name,
    )(*args)


def per_device(
    pooled,
    cotangent,
    compress_weight,
    fm_basis,
    fm_output,
    norm_gain,
    bag_ids,
    bag_lengths,
    slot_table,
    table_home,
):
    here = lax.axis_index("slot").astype(jnp.int32)
    at_slot = here.reshape(1)
    up_moves, far_moves, down_moves = (
        [(i, (i + step) % N_SLOT) for i in range(N_SLOT)] for step in (1, 2, 3)
    )
    own, to_after, to_far, to_before = make_messages(
        at_slot,
        pooled.reshape(N_SLOT, POOLED_ROWS, D),
        cotangent.reshape(N_SLOT, POOLED_ROWS, D),
        jnp.transpose(bag_ids, (0, 2, 1)),
        bag_lengths,
        slot_table.reshape(1, SLOT_DEV),
        table_home.reshape(1, -1),
    )
    from_far = lax.ppermute(to_far, "slot", far_moves)
    from_before = lax.ppermute(to_after, "slot", up_moves)
    from_after = lax.ppermute(to_before, "slot", down_moves)
    sent = run_layers(
        at_slot, own, from_before, from_far, from_after, fetch(compress_weight), fm_basis, fm_output, norm_gain
    )
    got = lax.all_to_all(sent, "dp", split_axis=0, concat_axis=0, tiled=True)
    me = lax.axis_index("grp").astype(jnp.int32)
    side = me ^ 1
    mirror = N_GRP - 1 - me
    across = side ^ 3
    far, after, before = (here + 2) % N_SLOT, (here + 1) % N_SLOT, (here + 3) % N_SLOT

    def blocks(groups, chunks):
        return jnp.stack([chunk * N_GRP + group for group in groups for chunk in chunks])

    half_a, half_b = (far, after), (here, before)
    side_moves = [(i, i ^ 1) for i in range(N_GRP)]
    mirror_moves = [(i, N_GRP - 1 - i) for i in range(N_GRP)]
    a_sent, *prepared = run_first_bags(blocks((side, across), half_a), got)
    a_got = lax.ppermute(a_sent, "grp", side_moves)
    b_sent = run_later_bags(blocks((mirror, across), half_b), prepared, "b_sent")
    b_got = lax.ppermute(b_sent, "grp", mirror_moves)
    a_kept = run_later_bags(blocks((me, mirror), half_a), prepared, "a_kept")
    part = ((2, *CHUNK), bf16)
    a_own, a_next = small_call(add_parts_kernel, "add_a", (part, part), a_kept, a_got)
    a_last = lax.ppermute(a_next, "grp", mirror_moves)
    b_blocks, a_own = lax.optimization_barrier((blocks((me, side), half_b), a_own))
    b_kept = run_later_bags(b_blocks, prepared, "b_kept")
    b_own, b_next = small_call(add_parts_kernel, "add_b", (part, part), b_kept, b_got)
    b_last = lax.ppermute(b_next, "grp", side_moves)
    chunk = (CHUNK, bf16)
    to_far, to_after = small_call(sum_a_kernel, "sum_a", (chunk, chunk), a_own, a_last)
    from_far = lax.ppermute(to_far, "slot", far_moves)
    from_before = lax.ppermute(to_after, "slot", up_moves)
    kept, to_before = small_call(sum_b_kernel, "sum_b", ((CHUNK, f32), chunk), b_own, b_last)
    from_after = lax.ppermute(to_before, "slot", down_moves)
    return small_call(final_kernel, "final_sum", ((CHUNK, f32),), kept, from_far, from_before, from_after)[0]


def solution(mesh):
    in_specs = (
        P(("dp", "grp"), "slot", None),
        P(("dp", "grp"), "slot", None),
        P(),
        P(),
        P(),
        P(),
        P(("dp", "grp"), "slot", None),
        P(("dp", "grp"), "slot"),
        P("slot"),
        P(),
    )
    out_specs = P("dp", ("slot", "grp"), None)
    return jax.shard_map(
        per_device, mesh=mesh, in_specs=in_specs, out_specs=out_specs, check_vma=False
    )
```

```python
import functools

import jax
import jax.numpy as jnp
from jax import lax
from jax.experimental import pallas as pl
from jax.experimental.pallas import tpu as pltpu
from jax.sharding import PartitionSpec as P

D = 128
LAYERS = 2
ROWS = 4096
TABLE_DEV = 2
BAG = 8
CAPACITY = 4
N_SLOT = 4
N_GRP = 4
DP = 64
SLOT_DEV = 128
SLOTS = 512
RANK = 32
PAIR = 2
ROW_BLOCK = 256
DEAD = 64
ID_ROWS = 32
POOLED_ROWS = PAIR * SLOT_DEV
MSG_ROWS = 2 * POOLED_ROWS + ID_ROWS + 16

norm_eps = 1e-05
f32 = jnp.float32
bf16 = jnp.bfloat16


ANY_SPEC = pl.BlockSpec(memory_space=pl.ANY)
VMEM_SPEC = pl.BlockSpec(memory_space=pltpu.VMEM)
SMEM_SPEC = pl.BlockSpec(memory_space=pltpu.SMEM)


def dot(a, b, ca=1, cb=0):
    return lax.dot_general(a, b, (((ca,), (cb,)), ((), ())), preferred_element_type=f32)


def iota(shape, dim):
    return lax.broadcasted_iota(jnp.int32, shape, dim)


def messages_kernel(place_ref, pooled_any, cotangent_any, ids_any, lengths_any, slot_ref, home_ref, *refs):
    out_refs, (x_ref, ids_ref, lengths_ref, sems, small_sems) = refs[:N_SLOT], refs[N_SLOT:]
    small = [
        pltpu.make_async_copy(ids_any, ids_ref, small_sems.at[0]),
        pltpu.make_async_copy(lengths_any, lengths_ref, small_sems.at[1]),
    ]
    for copy in small:
        copy.start()
    fetches = []
    for part, source in enumerate((pooled_any, cotangent_any)):
        rows = pl.ds(part * POOLED_ROWS, POOLED_ROWS)
        for r in range(N_SLOT):
            dest = place_ref[0] ^ r
            fetches.append(pltpu.make_async_copy(source.at[dest], x_ref.at[r, rows], sems.at[part, r]))
            fetches[-1].start()
    slots = slot_ref[...]
    hot = jnp.where(iota((SLOT_DEV, SLOT_DEV), 0) == slots, 1.0, 0.0).astype(bf16)
    homes = jnp.broadcast_to(home_ref[...].astype(f32), (8, SLOT_DEV)).astype(bf16)
    across = dot(homes, hot)[:1].astype(jnp.int32)
    down = dot(hot, homes, 0, 1)[:, :1].astype(jnp.int32)
    earlier = iota((SLOT_DEV, SLOT_DEV), 0) < iota((SLOT_DEV, SLOT_DEV), 1)
    same = (down // TABLE_DEV == across // TABLE_DEV) & earlier
    rank = jnp.sum(jnp.where(same, 1.0, 0.0), axis=0, keepdims=True)
    target = (across // TABLE_DEV * CAPACITY).astype(f32) + rank
    table = across % TABLE_DEV * 16
    marks = jnp.broadcast_to(target, (16, SLOT_DEV)).astype(bf16)
    entry = iota((BAG, SLOT_DEV), 0)
    for copy in small:
        copy.wait()
    for r in range(N_SLOT):
        dest = place_ref[0] ^ r
        parts = []
        for b in range(PAIR):
            ids = ids_ref[dest * PAIR + b]
            live = entry < lengths_ref[pl.ds(dest * PAIR + b, 1), :]
            parts.append((jnp.where(live, ids // ROW_BLOCK, DEAD) + table).astype(f32))
            parts.append((ids % ROW_BLOCK).astype(f32))
        x_ref[r, 2 * POOLED_ROWS : 2 * POOLED_ROWS + ID_ROWS] = jnp.concatenate(parts, axis=0).astype(bf16)
        x_ref[r, 2 * POOLED_ROWS + ID_ROWS :] = marks
    for copy in fetches:
        copy.wait()
    stores = [pltpu.make_async_copy(x_ref.at[r], out_refs[r], sems.at[2, r]) for r in range(N_SLOT)]
    for copy in stores:
        copy.start()
    for copy in stores:
        copy.wait()


def make_messages(place, *args):
    message = jax.ShapeDtypeStruct((MSG_ROWS, D), bf16)
    return pl.pallas_call(
        messages_kernel,
        out_shape=(message,) * N_SLOT,
        in_specs=[SMEM_SPEC] + [ANY_SPEC] * 4 + [VMEM_SPEC] * 2,
        out_specs=(ANY_SPEC,) * N_SLOT,
        scratch_shapes=[
            pltpu.VMEM((N_SLOT, MSG_ROWS, D), bf16),
            pltpu.VMEM((N_SLOT * PAIR, BAG, SLOT_DEV), jnp.int32),
            pltpu.VMEM((N_SLOT * PAIR, SLOT_DEV), jnp.int32),
            pltpu.SemaphoreType.DMA((3, N_SLOT)),
            pltpu.SemaphoreType.DMA((2,)),
        ],
        compiler_params=pltpu.CompilerParams(vmem_limit_bytes=56 << 20),
        cost_estimate=pl.CostEstimate(flops=1_000_000, bytes_accessed=2 << 20, transcendentals=0),
        name="messages",
    )(place, *args)


def layers_kernel(
    here_ref, own_ref, near_ref, mirror_ref, far_ref, compress_ref, basis_ref, output_ref, gain_ref, out_ref, x_ref
):
    for r, ref in enumerate((own_ref, near_ref, far_ref, mirror_ref)):
        x_ref[here_ref[0] ^ r] = ref[...]
    gain = gain_ref[...]
    pair_rows = POOLED_ROWS
    current = []
    upstream = []
    for b in range(PAIR):
        rows = slice(b * SLOT_DEV, (b + 1) * SLOT_DEV)
        current.append(jnp.concatenate([x_ref[k, rows, :] for k in range(N_SLOT)], axis=0))
        rows = slice(pair_rows + b * SLOT_DEV, pair_rows + (b + 1) * SLOT_DEV)
        upstream.append(jnp.concatenate([x_ref[k, rows, :] for k in range(N_SLOT)], axis=0))
    saved = []
    for layer in range(LAYERS):
        wide = jnp.concatenate(current, axis=1)
        coefficient = dot(basis_ref[layer], wide, 0, 0).astype(bf16)
        mixed = dot(compress_ref[layer], wide)
        following = []
        entry = []
        for b in range(PAIR):
            lanes = slice(b * D, (b + 1) * D)
            coeff = coefficient[:, lanes]
            feature = dot(current[b], coeff, 1, 1).astype(bf16)
            total = current[b].astype(f32) + dot(feature, output_ref[layer]) + mixed[:, lanes]
            mean = jnp.mean(total, axis=1, keepdims=True)
            centered = total - mean
            variance = jnp.mean(centered * centered, axis=1, keepdims=True)
            inv_std = lax.rsqrt(variance + norm_eps)
            normed = centered * inv_std
            entry.append((current[b], normed, inv_std, coeff))
            following.append((normed * gain[layer : layer + 1]).astype(bf16))
        saved.append(entry)
        current = following
    for layer in reversed(range(LAYERS)):
        lows = []
        local = []
        grad_feats = []
        for b in range(PAIR):
            inputs, normed, inv_std, coeff = saved[layer][b]
            scaled = upstream[b].astype(f32) * gain[layer : layer + 1]
            grad_sum = inv_std * (
                scaled
                - jnp.mean(scaled, axis=1, keepdims=True)
                - normed * jnp.mean(scaled * normed, axis=1, keepdims=True)
            )
            low = grad_sum.astype(bf16)
            grad_feat = dot(low, output_ref[layer], 1, 1).astype(bf16)
            local.append(grad_sum + dot(grad_feat, coeff))
            lows.append(low)
            grad_feats.append(grad_feat)
        linear = dot(compress_ref[layer], jnp.concatenate(lows, axis=1), 0, 0)
        basis_twice = jnp.concatenate([basis_ref[layer], basis_ref[layer]], axis=1)
        for b in range(PAIR):
            grad_coeff = dot(grad_feats[b], saved[layer][b][0], 0, 0)
            high = grad_coeff.astype(bf16)
            rest = (grad_coeff - high.astype(f32)).astype(bf16)
            basis_part = dot(basis_twice, jnp.concatenate([high, rest], axis=0))
            upstream[b] = (local[b] + linear[:, b * D : (b + 1) * D] + basis_part).astype(bf16)
    shape = (DP * PAIR * CAPACITY, PAIR * SLOT_DEV)
    row = iota(shape, 0)
    row_key = row // (PAIR * CAPACITY) * CAPACITY + row % CAPACITY + row // CAPACITY % PAIR * 1024
    sample_key = iota((1, PAIR * SLOT_DEV), 1) // SLOT_DEV * 1024
    targets = []
    for k in range(N_SLOT):
        target = x_ref[k, 2 * pair_rows + ID_ROWS : 2 * pair_rows + ID_ROWS + 16, :]
        target = target[:1].astype(f32).astype(jnp.int32)
        targets.append(target)
        column_key = jnp.concatenate([target] * PAIR, axis=1) + sample_key
        placing = jnp.where(row_key == column_key, 1.0, 0.0).astype(bf16)
        rows = slice(k * SLOT_DEV, (k + 1) * SLOT_DEV)
        values = jnp.concatenate([u[rows] for u in upstream], axis=0)
        out_ref[:, k] = dot(placing, values).astype(bf16).reshape(DP, PAIR * CAPACITY, D)
    shape = (DP * 8, SLOTS)
    row = iota(shape, 0)
    row_key = row // 8 * CAPACITY + row % 8 * 1024
    column_key = jnp.concatenate([targets[k] + k * 1024 for k in range(N_SLOT)], axis=1)
    unpacked = jnp.concatenate(
        [x_ref[k, 2 * pair_rows : 2 * pair_rows + ID_ROWS, :] for k in range(N_SLOT)], axis=1
    )
    unpacked = jnp.concatenate([unpacked] * CAPACITY, axis=0)
    rank_lane = iota((1, D), 1) // 32
    ids = jnp.zeros((DP * 8, D), f32)
    for rank in range(CAPACITY):
        placing = jnp.where(row_key + rank == column_key, 1.0, 0.0).astype(bf16)
        ids = ids + jnp.where(rank_lane == rank, dot(placing, unpacked, 1, 1), 0.0)
    out_ref[:, N_SLOT] = ids.astype(bf16).reshape(DP, 8, D)


def fetch_kernel(source_any, out_ref, sem):
    copy = pltpu.make_async_copy(source_any, out_ref, sem)
    copy.start()
    copy.wait()


def fetch(source):
    return pl.pallas_call(
        fetch_kernel,
        out_shape=jax.ShapeDtypeStruct(source.shape, source.dtype),
        in_specs=[ANY_SPEC],
        out_specs=VMEM_SPEC,
        scratch_shapes=[pltpu.SemaphoreType.DMA],
        compiler_params=pltpu.CompilerParams(vmem_limit_bytes=8 << 20),
        cost_estimate=pl.CostEstimate(flops=0, bytes_accessed=2 << 20, transcendentals=0),
        name="fetch_weights",
    )(source)


def run_layers(here, *args):
    return pl.pallas_call(
        layers_kernel,
        out_shape=jax.ShapeDtypeStruct((DP, N_SLOT + 1, 8, D), bf16),
        in_specs=[SMEM_SPEC] + [VMEM_SPEC] * len(args),
        out_specs=VMEM_SPEC,
        scratch_shapes=[pltpu.VMEM((N_SLOT, MSG_ROWS, D), bf16)],
        compiler_params=pltpu.CompilerParams(vmem_limit_bytes=20 << 20),
        cost_estimate=pl.CostEstimate(flops=2_000_000_000, bytes_accessed=4 << 20, transcendentals=4096),
        name="layers",
    )(here, *args)


def prepare_bags(got_ref, wide_ref, grads_ref, high_ref, low_ref):
    bags = PAIR * DP
    shape = (DP * 8, N_SLOT * bags)
    row = iota(shape, 0)
    lane = iota(shape, 1)
    pick = (row // 8 == lane % DP) & (row % 8 == lane // bags)
    ids = dot(
        got_ref[:, N_SLOT].reshape(DP * 8, D), jnp.where(pick, 1.0, 0.0).astype(bf16), 0, 0
    )
    first_sample = iota((1, bags), 1) < DP
    for k in range(N_SLOT):
        wide_ref[...] = got_ref[:, k].astype(f32).reshape(DP * 8, D)
        for rank in range(CAPACITY):
            cap = k * CAPACITY + rank
            both = ids[rank * 32 : (rank + 1) * 32, k * bags : (k + 1) * bags]
            own = jnp.where(first_sample, both[:16], both[16:])
            high, low = own[:8], own[8:]
            alive = jnp.where(high >= DEAD, high - DEAD, high)[:1]
            table = jnp.where(jnp.max(alive, axis=1, keepdims=True) >= 16, 1.0, 0.0)
            half = cap % 2
            lanes = slice(half * bags, (half + 1) * bags)
            high_ref[cap // 2, :, lanes] = high - 16.0 * table
            low_ref[cap // 2, :, lanes] = low
            values = jnp.concatenate(
                [wide_ref[pl.ds(b * CAPACITY + rank, DP, stride=8), :] for b in range(PAIR)], axis=0
            )
            rows = slice(half * bags, (half + 1) * bags)
            grads_ref[cap // 2, rows, :D] = (values * (1.0 - table)).astype(bf16)
            grads_ref[cap // 2, rows, D:] = (values * table).astype(bf16)


def add_rows(blocks_ref, out_ref, grads_ref, high_ref, low_ref):
    lanes = 2 * PAIR * DP
    rows_of = iota((ROW_BLOCK, lanes), 0).astype(f32).astype(bf16)
    zero = jnp.zeros((), bf16)

    def spread(row):
        row = jnp.broadcast_to(row, (16, lanes)).astype(bf16)
        return jnp.broadcast_to(row[None], (ROW_BLOCK // 16, 16, lanes)).reshape(ROW_BLOCK, lanes)

    def block(index, carry):
        first = blocks_ref[2 * index].astype(f32)
        second = blocks_ref[2 * index + 1].astype(f32)
        totals = [jnp.zeros((ROW_BLOCK, 2 * D), f32)] * 2
        for p in range(N_SLOT * CAPACITY // 2):
            high = high_ref[p]
            low = low_ref[p]
            weight = jnp.where(high == first, 1.0, jnp.where(high == second, 16.0, 0.0))
            packed = jnp.zeros((ROW_BLOCK, lanes), bf16)
            for j in range(BAG):
                hit = rows_of == spread(low[j : j + 1])
                packed = packed + jnp.where(hit, spread(weight[j : j + 1]), zero)
            upper = ((packed - 7.5) + 3072.0) - 3072.0
            totals = [totals[0] + dot(packed - upper, grads_ref[p]), totals[1] + dot(upper, grads_ref[p])]
        for c, scale in ((0, 1.0), (1, 0.0625)):
            total = totals[c] * scale
            out_ref[index, c, 0] = total[:, :D].astype(bf16)
            out_ref[index, c, 1] = total[:, D:].astype(bf16)
        return carry

    lax.fori_loop(0, 2, block, 0)


def first_bags_kernel(blocks_ref, got_ref, out_ref, grads_ref, high_ref, low_ref, wide_ref):
    prepare_bags(got_ref, wide_ref, grads_ref, high_ref, low_ref)
    add_rows(blocks_ref, out_ref, grads_ref, high_ref, low_ref)


def later_bags_kernel(blocks_ref, grads_ref, high_ref, low_ref, out_ref):
    add_rows(blocks_ref, out_ref, grads_ref, high_ref, low_ref)


BAGS_COST = pl.CostEstimate(flops=200_000_000, bytes_accessed=1 << 20, transcendentals=0)
ADD_COST = pl.CostEstimate(flops=1_000_000, bytes_accessed=1 << 20, transcendentals=0)
CHUNK = (TABLE_DEV, ROW_BLOCK, D)


def run_first_bags(blocks, got):
    pairs = N_SLOT * CAPACITY // 2
    lanes = 2 * PAIR * DP
    return pl.pallas_call(
        first_bags_kernel,
        out_shape=(
            jax.ShapeDtypeStruct((2, 2, *CHUNK), bf16),
            jax.ShapeDtypeStruct((pairs, lanes, 2 * D), bf16),
            jax.ShapeDtypeStruct((pairs, BAG, lanes), f32),
            jax.ShapeDtypeStruct((pairs, BAG, lanes), f32),
        ),
        in_specs=[SMEM_SPEC, VMEM_SPEC],
        out_specs=(VMEM_SPEC,) * 4,
        scratch_shapes=[pltpu.VMEM((DP * 8, D), f32)],
        compiler_params=pltpu.CompilerParams(vmem_limit_bytes=24 << 20),
        cost_estimate=BAGS_COST,
        name="first_bags",
    )(blocks, got)


def run_later_bags(blocks, prepared, name):
    return pl.pallas_call(
        later_bags_kernel,
        out_shape=jax.ShapeDtypeStruct((2, 2, *CHUNK), bf16),
        in_specs=[SMEM_SPEC] + [VMEM_SPEC] * 3,
        out_specs=VMEM_SPEC,
        compiler_params=pltpu.CompilerParams(vmem_limit_bytes=24 << 20),
        cost_estimate=BAGS_COST,
        name=name,
    )(blocks, *prepared)


def wide_sum(*refs):
    total = refs[0][...].astype(f32)
    for ref in refs[1:]:
        total = total + ref[...].astype(f32)
    return total


def add_parts_kernel(kept_ref, got_ref, own_ref, sent_ref):
    own_ref[...] = wide_sum(kept_ref.at[0], got_ref.at[0]).astype(bf16)
    sent_ref[...] = wide_sum(kept_ref.at[1], got_ref.at[1]).astype(bf16)


def sum_a_kernel(own_ref, got_ref, near_ref, mirror_ref):
    near_ref[...] = wide_sum(own_ref.at[0], got_ref.at[0]).astype(bf16)
    mirror_ref[...] = wide_sum(own_ref.at[1], got_ref.at[1]).astype(bf16)


def sum_b_kernel(own_ref, got_ref, kept_ref, far_ref):
    kept_ref[...] = wide_sum(own_ref.at[0], got_ref.at[0])
    far_ref[...] = wide_sum(own_ref.at[1], got_ref.at[1]).astype(bf16)


def final_kernel(kept_ref, near_ref, mirror_ref, far_ref, out_ref):
    out_ref[...] = wide_sum(kept_ref, near_ref, mirror_ref, far_ref)


def small_call(kernel, name, shapes, *args):
    outs = tuple(jax.ShapeDtypeStruct(shape, dtype) for shape, dtype in shapes)
    return pl.pallas_call(
        kernel,
        out_shape=outs,
        in_specs=[VMEM_SPEC] * len(args),
        out_specs=(VMEM_SPEC,) * len(outs),
        compiler_params=pltpu.CompilerParams(vmem_limit_bytes=8 << 20),
        cost_estimate=ADD_COST,
        name=name,
    )(*args)


def per_device(
    pooled,
    cotangent,
    compress_weight,
    fm_basis,
    fm_output,
    norm_gain,
    bag_ids,
    bag_lengths,
    slot_table,
    table_home,
):
    here = lax.axis_index("slot").astype(jnp.int32)
    at_slot = here.reshape(1)
    swaps = [[(i, i ^ r) for i in range(N_SLOT)] for r in range(N_SLOT)]
    own, near, far, mirror = make_messages(
        at_slot,
        pooled.reshape(N_SLOT, POOLED_ROWS, D),
        cotangent.reshape(N_SLOT, POOLED_ROWS, D),
        jnp.transpose(bag_ids, (0, 2, 1)),
        bag_lengths,
        slot_table.reshape(1, SLOT_DEV),
        table_home.reshape(1, -1),
    )
    near = lax.ppermute(near, "slot", swaps[1])
    mirror = lax.ppermute(mirror, "slot", swaps[3])
    far = lax.ppermute(far, "slot", swaps[2])
    sent = run_layers(
        at_slot, own, near, mirror, far, fetch(compress_weight), fm_basis, fm_output, norm_gain
    )
    got = lax.all_to_all(sent, "dp", split_axis=0, concat_axis=0, tiled=True)
    me = lax.axis_index("grp").astype(jnp.int32)
    side = me ^ 1
    opposite = N_GRP - 1 - me
    across = side ^ 3

    def blocks(groups, chunks):
        return jnp.stack([chunk * N_GRP + group for group in groups for chunk in chunks])

    half_a, half_b = (here ^ 1, here ^ 3), (here, here ^ 2)
    side_moves = [(i, i ^ 1) for i in range(N_GRP)]
    mirror_moves = [(i, N_GRP - 1 - i) for i in range(N_GRP)]
    a_sent, *prepared = run_first_bags(blocks((side, across), half_a), got)
    a_got = lax.ppermute(a_sent, "grp", side_moves)
    b_sent = run_later_bags(blocks((opposite, across), half_b), prepared, "b_sent")
    b_got = lax.ppermute(b_sent, "grp", mirror_moves)
    a_kept = run_later_bags(blocks((me, opposite), half_a), prepared, "a_kept")
    part = ((2, *CHUNK), bf16)
    a_own, a_next = small_call(add_parts_kernel, "add_a", (part, part), a_kept, a_got)
    a_last = lax.ppermute(a_next, "grp", mirror_moves)
    b_blocks, a_own = lax.optimization_barrier((blocks((me, side), half_b), a_own))
    b_kept = run_later_bags(b_blocks, prepared, "b_kept")
    b_own, b_next = small_call(add_parts_kernel, "add_b", (part, part), b_kept, b_got)
    b_last = lax.ppermute(b_next, "grp", side_moves)
    chunk = (CHUNK, bf16)
    near, mirror = small_call(sum_a_kernel, "sum_a", (chunk, chunk), a_own, a_last)
    near = lax.ppermute(near, "slot", swaps[1])
    mirror = lax.ppermute(mirror, "slot", swaps[3])
    kept, far = small_call(sum_b_kernel, "sum_b", ((CHUNK, f32), chunk), b_own, b_last)
    far = lax.ppermute(far, "slot", swaps[2])
    return small_call(final_kernel, "final_sum", ((CHUNK, f32),), kept, near, mirror, far)[0]


def solution(mesh):
    in_specs = (
        P(("dp", "grp"), "slot", None),
        P(("dp", "grp"), "slot", None),
        P(),
        P(),
        P(),
        P(),
        P(("dp", "grp"), "slot", None),
        P(("dp", "grp"), "slot"),
        P("slot"),
        P(),
    )
    out_specs = P("dp", ("slot", "grp"), None)
    return jax.shard_map(
        per_device, mesh=mesh, in_specs=in_specs, out_specs=out_specs, check_vma=False
    )
```

```python
import functools

import jax
import jax.numpy as jnp
from jax import lax
from jax.experimental import pallas as pl
from jax.experimental.pallas import tpu as pltpu
from jax.sharding import PartitionSpec as P

D = 128
LAYERS = 2
ROWS = 4096
TABLE_DEV = 2
BAG = 8
CAPACITY = 4
N_SLOT = 4
N_GRP = 4
DP = 64
SLOT_DEV = 128
SLOTS = 512
RANK = 32
PAIR = 2
ROW_BLOCK = 256
DEAD = 64
ID_ROWS = 32
POOLED_ROWS = PAIR * SLOT_DEV
MSG_ROWS = 2 * POOLED_ROWS + ID_ROWS + 16

norm_eps = 1e-05
f32 = jnp.float32
bf16 = jnp.bfloat16


ANY_SPEC = pl.BlockSpec(memory_space=pl.ANY)
VMEM_SPEC = pl.BlockSpec(memory_space=pltpu.VMEM)
SMEM_SPEC = pl.BlockSpec(memory_space=pltpu.SMEM)


def dot(a, b, ca=1, cb=0):
    return lax.dot_general(a, b, (((ca,), (cb,)), ((), ())), preferred_element_type=f32)


def iota(shape, dim):
    return lax.broadcasted_iota(jnp.int32, shape, dim)


def messages_kernel(place_ref, pooled_any, cotangent_any, ids_any, lengths_any, slot_ref, home_ref, *refs):
    out_refs, (x_ref, ids_ref, lengths_ref, sems, small_sems) = refs[:N_SLOT], refs[N_SLOT:]
    small = [
        pltpu.make_async_copy(ids_any, ids_ref, small_sems.at[0]),
        pltpu.make_async_copy(lengths_any, lengths_ref, small_sems.at[1]),
    ]
    for copy in small:
        copy.start()
    fetches = []
    for part, source in enumerate((pooled_any, cotangent_any)):
        rows = pl.ds(part * POOLED_ROWS, POOLED_ROWS)
        for r in range(N_SLOT):
            dest = place_ref[0] ^ r
            fetches.append(pltpu.make_async_copy(source.at[dest], x_ref.at[r, rows], sems.at[part, r]))
            fetches[-1].start()
    slots = slot_ref[...]
    hot = jnp.where(iota((SLOT_DEV, SLOT_DEV), 0) == slots, 1.0, 0.0).astype(bf16)
    homes = jnp.broadcast_to(home_ref[...].astype(f32), (8, SLOT_DEV)).astype(bf16)
    across = dot(homes, hot)[:1].astype(jnp.int32)
    down = dot(hot, homes, 0, 1)[:, :1].astype(jnp.int32)
    earlier = iota((SLOT_DEV, SLOT_DEV), 0) < iota((SLOT_DEV, SLOT_DEV), 1)
    same = (down // TABLE_DEV == across // TABLE_DEV) & earlier
    rank = jnp.sum(jnp.where(same, 1.0, 0.0), axis=0, keepdims=True)
    target = (across // TABLE_DEV * CAPACITY).astype(f32) + rank
    table = across % TABLE_DEV * 16
    marks = jnp.broadcast_to(target, (16, SLOT_DEV)).astype(bf16)
    entry = iota((BAG, SLOT_DEV), 0)
    for copy in small:
        copy.wait()
    for r in range(N_SLOT):
        dest = place_ref[0] ^ r
        parts = []
        for b in range(PAIR):
            ids = ids_ref[dest * PAIR + b]
            live = entry < lengths_ref[pl.ds(dest * PAIR + b, 1), :]
            parts.append((jnp.where(live, ids // ROW_BLOCK, DEAD) + table).astype(f32))
            parts.append((ids % ROW_BLOCK).astype(f32))
        x_ref[r, 2 * POOLED_ROWS : 2 * POOLED_ROWS + ID_ROWS] = jnp.concatenate(parts, axis=0).astype(bf16)
        x_ref[r, 2 * POOLED_ROWS + ID_ROWS :] = marks
    stores = []
    for r in (1, 3, 2, 0):
        fetches[r].wait()
        fetches[N_SLOT + r].wait()
        stores.append(pltpu.make_async_copy(x_ref.at[r], out_refs[r], sems.at[2, r]))
        stores[-1].start()
    for copy in stores:
        copy.wait()


def make_messages(place, *args):
    message = jax.ShapeDtypeStruct((MSG_ROWS, D), bf16)
    return pl.pallas_call(
        messages_kernel,
        out_shape=(message,) * N_SLOT,
        in_specs=[SMEM_SPEC] + [ANY_SPEC] * 4 + [VMEM_SPEC] * 2,
        out_specs=(ANY_SPEC,) * N_SLOT,
        scratch_shapes=[
            pltpu.VMEM((N_SLOT, MSG_ROWS, D), bf16),
            pltpu.VMEM((N_SLOT * PAIR, BAG, SLOT_DEV), jnp.int32),
            pltpu.VMEM((N_SLOT * PAIR, SLOT_DEV), jnp.int32),
            pltpu.SemaphoreType.DMA((3, N_SLOT)),
            pltpu.SemaphoreType.DMA((2,)),
        ],
        compiler_params=pltpu.CompilerParams(vmem_limit_bytes=56 << 20),
        cost_estimate=pl.CostEstimate(flops=1_000_000, bytes_accessed=2 << 20, transcendentals=0),
        name="messages",
    )(place, *args)


def layers_kernel(
    here_ref, own_ref, near_ref, mirror_ref, far_ref, compress_ref, turned_ref, basis_ref, output_ref, gain_ref, out_ref, x_ref
):
    for r, ref in enumerate((own_ref, near_ref, far_ref, mirror_ref)):
        x_ref[here_ref[0] ^ r] = ref[...]
    gain = gain_ref[...]
    pair_rows = POOLED_ROWS
    current = []
    upstream = []
    for b in range(PAIR):
        rows = slice(b * SLOT_DEV, (b + 1) * SLOT_DEV)
        current.append(jnp.concatenate([x_ref[k, rows, :] for k in range(N_SLOT)], axis=0))
        rows = slice(pair_rows + b * SLOT_DEV, pair_rows + (b + 1) * SLOT_DEV)
        upstream.append(jnp.concatenate([x_ref[k, rows, :] for k in range(N_SLOT)], axis=0))
    saved = []
    for layer in range(LAYERS):
        wide = jnp.concatenate(current, axis=1)
        coefficient = dot(basis_ref[layer], wide, 0, 0).astype(bf16)
        mixed = dot(compress_ref[layer], wide)
        following = []
        entry = []
        for b in range(PAIR):
            lanes = slice(b * D, (b + 1) * D)
            coeff = coefficient[:, lanes]
            feature = dot(current[b], coeff, 1, 1).astype(bf16)
            total = current[b].astype(f32) + dot(feature, output_ref[layer]) + mixed[:, lanes]
            mean = jnp.mean(total, axis=1, keepdims=True)
            centered = total - mean
            variance = jnp.mean(centered * centered, axis=1, keepdims=True)
            inv_std = lax.rsqrt(variance + norm_eps)
            normed = centered * inv_std
            entry.append((current[b], normed, inv_std, coeff))
            following.append((normed * gain[layer : layer + 1]).astype(bf16))
        saved.append(entry)
        current = following
    for layer in reversed(range(LAYERS)):
        lows = []
        local = []
        grad_feats = []
        for b in range(PAIR):
            inputs, normed, inv_std, coeff = saved[layer][b]
            scaled = upstream[b].astype(f32) * gain[layer : layer + 1]
            grad_sum = inv_std * (
                scaled
                - jnp.mean(scaled, axis=1, keepdims=True)
                - normed * jnp.mean(scaled * normed, axis=1, keepdims=True)
            )
            low = grad_sum.astype(bf16)
            grad_feat = dot(low, output_ref[layer], 1, 1).astype(bf16)
            local.append(grad_sum + dot(grad_feat, coeff))
            lows.append(low)
            grad_feats.append(grad_feat)
        linear = dot(turned_ref[layer], jnp.concatenate(lows, axis=1))
        basis_twice = jnp.concatenate([basis_ref[layer], basis_ref[layer]], axis=1)
        for b in range(PAIR):
            grad_coeff = dot(grad_feats[b], saved[layer][b][0], 0, 0)
            high = grad_coeff.astype(bf16)
            rest = (grad_coeff - high.astype(f32)).astype(bf16)
            basis_part = dot(basis_twice, jnp.concatenate([high, rest], axis=0))
            upstream[b] = (local[b] + linear[:, b * D : (b + 1) * D] + basis_part).astype(bf16)
    shape = (DP * PAIR * CAPACITY, PAIR * SLOT_DEV)
    row = iota(shape, 0)
    row_key = row // (PAIR * CAPACITY) * CAPACITY + row % CAPACITY + row // CAPACITY % PAIR * 1024
    sample_key = iota((1, PAIR * SLOT_DEV), 1) // SLOT_DEV * 1024
    targets = []
    for k in range(N_SLOT):
        target = x_ref[k, 2 * pair_rows + ID_ROWS : 2 * pair_rows + ID_ROWS + 16, :]
        target = target[:1].astype(f32).astype(jnp.int32)
        targets.append(target)
        column_key = jnp.concatenate([target] * PAIR, axis=1) + sample_key
        placing = jnp.where(row_key == column_key, 1.0, 0.0).astype(bf16)
        rows = slice(k * SLOT_DEV, (k + 1) * SLOT_DEV)
        values = jnp.concatenate([u[rows] for u in upstream], axis=0)
        out_ref[:, k] = dot(placing, values).astype(bf16).reshape(DP, PAIR * CAPACITY, D)
    shape = (DP * 8, SLOTS)
    row = iota(shape, 0)
    row_key = row // 8 + row % 8 * 1024
    targets = jnp.concatenate(targets, axis=1)
    column_key = targets // CAPACITY + iota((1, SLOTS), 1) // SLOT_DEV * 1024
    unpacked = jnp.concatenate(
        [x_ref[k, 2 * pair_rows : 2 * pair_rows + ID_ROWS, :] for k in range(N_SLOT)], axis=1
    )
    unpacked = jnp.concatenate([unpacked.astype(f32)] * CAPACITY, axis=0)
    picked = iota((D, SLOTS), 0) // ID_ROWS == targets % CAPACITY
    unpacked = jnp.where(picked, unpacked, 0.0).astype(bf16)
    ids = dot(jnp.where(row_key == column_key, 1.0, 0.0).astype(bf16), unpacked, 1, 1)
    out_ref[:, N_SLOT] = ids.astype(bf16).reshape(DP, 8, D)


def weights_kernel(source_ref, out_ref, turned_ref):
    for layer in range(LAYERS):
        out_ref[layer] = source_ref[layer]
        turned_ref[layer] = source_ref[layer].T


def prepare_weights(source):
    shape = jax.ShapeDtypeStruct(source.shape, source.dtype)
    return pl.pallas_call(
        weights_kernel,
        out_shape=(shape, shape),
        in_specs=[VMEM_SPEC],
        out_specs=(VMEM_SPEC, VMEM_SPEC),
        compiler_params=pltpu.CompilerParams(vmem_limit_bytes=12 << 20),
        cost_estimate=pl.CostEstimate(flops=0, bytes_accessed=3 << 20, transcendentals=0),
        name="prepare_weights",
    )(source)


def run_layers(here, *args):
    return pl.pallas_call(
        layers_kernel,
        out_shape=jax.ShapeDtypeStruct((DP, N_SLOT + 1, 8, D), bf16),
        in_specs=[SMEM_SPEC] + [VMEM_SPEC] * len(args),
        out_specs=VMEM_SPEC,
        scratch_shapes=[pltpu.VMEM((N_SLOT, MSG_ROWS, D), bf16)],
        compiler_params=pltpu.CompilerParams(vmem_limit_bytes=20 << 20),
        cost_estimate=pl.CostEstimate(flops=2_000_000_000, bytes_accessed=4 << 20, transcendentals=4096),
        name="layers",
    )(here, *args)


def prepare_bags(got_ref, wide_ref, grads_ref, high_ref, low_ref):
    bags = PAIR * DP
    shape = (DP * 8, N_SLOT * bags)
    row = iota(shape, 0)
    lane = iota(shape, 1)
    pick = (row // 8 == lane % DP) & (row % 8 == lane // bags)
    ids = dot(
        got_ref[:, N_SLOT].reshape(DP * 8, D), jnp.where(pick, 1.0, 0.0).astype(bf16), 0, 0
    )
    first_sample = iota((1, bags), 1) < DP
    for k in range(N_SLOT):
        wide_ref[...] = got_ref[:, k].astype(f32).reshape(DP * 8, D)
        for rank in range(CAPACITY):
            cap = k * CAPACITY + rank
            both = ids[rank * 32 : (rank + 1) * 32, k * bags : (k + 1) * bags]
            own = jnp.where(first_sample, both[:16], both[16:])
            high, low = own[:8], own[8:]
            alive = jnp.where(high >= DEAD, high - DEAD, high)[:1]
            table = jnp.where(jnp.max(alive, axis=1, keepdims=True) >= 16, 1.0, 0.0)
            half = cap % 2
            lanes = slice(half * bags, (half + 1) * bags)
            high_ref[cap // 2, :, lanes] = high - 16.0 * table
            low_ref[cap // 2, :, lanes] = low
            values = jnp.concatenate(
                [wide_ref[pl.ds(b * CAPACITY + rank, DP, stride=8), :] for b in range(PAIR)], axis=0
            )
            rows = slice(half * bags, (half + 1) * bags)
            grads_ref[cap // 2, rows, :D] = (values * (1.0 - table)).astype(bf16)
            grads_ref[cap // 2, rows, D:] = (values * table).astype(bf16)


def add_rows(blocks_ref, out_ref, grads_ref, high_ref, low_ref):
    lanes = 2 * PAIR * DP
    rows_of = iota((ROW_BLOCK, lanes), 0).astype(f32).astype(bf16)
    zero = jnp.zeros((), bf16)

    def spread(row):
        row = jnp.broadcast_to(row, (16, lanes)).astype(bf16)
        return jnp.broadcast_to(row[None], (ROW_BLOCK // 16, 16, lanes)).reshape(ROW_BLOCK, lanes)

    def block(index, carry):
        first = blocks_ref[2 * index].astype(f32)
        second = blocks_ref[2 * index + 1].astype(f32)
        totals = [jnp.zeros((ROW_BLOCK, 2 * D), f32)] * 2
        for p in range(N_SLOT * CAPACITY // 2):
            high = high_ref[p]
            low = low_ref[p]
            weight = jnp.where(high == first, 1.0, jnp.where(high == second, 16.0, 0.0))
            packed = jnp.zeros((ROW_BLOCK, lanes), bf16)
            for j in range(BAG):
                hit = rows_of == spread(low[j : j + 1])
                packed = packed + jnp.where(hit, spread(weight[j : j + 1]), zero)
            upper = ((packed - 7.5) + 3072.0) - 3072.0
            totals = [totals[0] + dot(packed - upper, grads_ref[p]), totals[1] + dot(upper, grads_ref[p])]
        for c, scale in ((0, 1.0), (1, 0.0625)):
            total = totals[c] * scale
            out_ref[index, c, 0] = total[:, :D].astype(bf16)
            out_ref[index, c, 1] = total[:, D:].astype(bf16)
        return carry

    lax.fori_loop(0, 2, block, 0)


def first_bags_kernel(blocks_ref, got_ref, out_ref, grads_ref, high_ref, low_ref, wide_ref):
    prepare_bags(got_ref, wide_ref, grads_ref, high_ref, low_ref)
    add_rows(blocks_ref, out_ref, grads_ref, high_ref, low_ref)


def later_bags_kernel(blocks_ref, grads_ref, high_ref, low_ref, out_ref):
    add_rows(blocks_ref, out_ref, grads_ref, high_ref, low_ref)


BAGS_COST = pl.CostEstimate(flops=200_000_000, bytes_accessed=1 << 20, transcendentals=0)
ADD_COST = pl.CostEstimate(flops=1_000_000, bytes_accessed=1 << 20, transcendentals=0)
CHUNK = (TABLE_DEV, ROW_BLOCK, D)


def run_first_bags(blocks, got):
    pairs = N_SLOT * CAPACITY // 2
    lanes = 2 * PAIR * DP
    return pl.pallas_call(
        first_bags_kernel,
        out_shape=(
            jax.ShapeDtypeStruct((2, 2, *CHUNK), bf16),
            jax.ShapeDtypeStruct((pairs, lanes, 2 * D), bf16),
            jax.ShapeDtypeStruct((pairs, BAG, lanes), f32),
            jax.ShapeDtypeStruct((pairs, BAG, lanes), f32),
        ),
        in_specs=[SMEM_SPEC, VMEM_SPEC],
        out_specs=(VMEM_SPEC,) * 4,
        scratch_shapes=[pltpu.VMEM((DP * 8, D), f32)],
        compiler_params=pltpu.CompilerParams(vmem_limit_bytes=24 << 20),
        cost_estimate=BAGS_COST,
        name="first_bags",
    )(blocks, got)


def run_later_bags(blocks, prepared, name):
    return pl.pallas_call(
        later_bags_kernel,
        out_shape=jax.ShapeDtypeStruct((2, 2, *CHUNK), bf16),
        in_specs=[SMEM_SPEC] + [VMEM_SPEC] * 3,
        out_specs=VMEM_SPEC,
        compiler_params=pltpu.CompilerParams(vmem_limit_bytes=24 << 20),
        cost_estimate=BAGS_COST,
        name=name,
    )(blocks, *prepared)


def wide_sum(*refs):
    total = refs[0][...].astype(f32)
    for ref in refs[1:]:
        total = total + ref[...].astype(f32)
    return total


def add_parts_kernel(kept_ref, got_ref, own_ref, sent_ref):
    own_ref[...] = wide_sum(kept_ref.at[0], got_ref.at[0]).astype(bf16)
    sent_ref[...] = wide_sum(kept_ref.at[1], got_ref.at[1]).astype(bf16)


def sum_a_kernel(own_ref, got_ref, near_ref, mirror_ref):
    near_ref[...] = wide_sum(own_ref.at[0], got_ref.at[0]).astype(bf16)
    mirror_ref[...] = wide_sum(own_ref.at[1], got_ref.at[1]).astype(bf16)


def sum_b_kernel(own_ref, got_ref, kept_ref, far_ref):
    kept_ref[...] = wide_sum(own_ref.at[0], got_ref.at[0])
    far_ref[...] = wide_sum(own_ref.at[1], got_ref.at[1]).astype(bf16)


def final_kernel(kept_ref, near_ref, mirror_ref, far_ref, out_ref):
    out_ref[...] = wide_sum(kept_ref, near_ref, mirror_ref, far_ref)


def small_call(kernel, name, shapes, *args):
    outs = tuple(jax.ShapeDtypeStruct(shape, dtype) for shape, dtype in shapes)
    return pl.pallas_call(
        kernel,
        out_shape=outs,
        in_specs=[VMEM_SPEC] * len(args),
        out_specs=(VMEM_SPEC,) * len(outs),
        compiler_params=pltpu.CompilerParams(vmem_limit_bytes=8 << 20),
        cost_estimate=ADD_COST,
        name=name,
    )(*args)


def per_device(
    pooled,
    cotangent,
    compress_weight,
    fm_basis,
    fm_output,
    norm_gain,
    bag_ids,
    bag_lengths,
    slot_table,
    table_home,
):
    here = lax.axis_index("slot").astype(jnp.int32)
    at_slot = here.reshape(1)
    swaps = [[(i, i ^ r) for i in range(N_SLOT)] for r in range(N_SLOT)]
    own, near, far, mirror = make_messages(
        at_slot,
        pooled.reshape(N_SLOT, POOLED_ROWS, D),
        cotangent.reshape(N_SLOT, POOLED_ROWS, D),
        jnp.transpose(bag_ids, (0, 2, 1)),
        bag_lengths,
        slot_table.reshape(1, SLOT_DEV),
        table_home.reshape(1, -1),
    )
    near = lax.ppermute(near, "slot", swaps[1])
    mirror = lax.ppermute(mirror, "slot", swaps[3])
    far = lax.ppermute(far, "slot", swaps[2])
    sent = run_layers(
        at_slot, own, near, mirror, far, *prepare_weights(compress_weight), fm_basis, fm_output, norm_gain
    )
    got = lax.all_to_all(sent, "dp", split_axis=0, concat_axis=0, tiled=True)
    me = lax.axis_index("grp").astype(jnp.int32)
    side = me ^ 1
    opposite = N_GRP - 1 - me
    across = side ^ 3

    def blocks(groups, chunks):
        return jnp.stack([chunk * N_GRP + group for group in groups for chunk in chunks])

    half_a, half_b = (here ^ 1, here ^ 3), (here, here ^ 2)
    side_moves = [(i, i ^ 1) for i in range(N_GRP)]
    mirror_moves = [(i, N_GRP - 1 - i) for i in range(N_GRP)]
    a_sent, *prepared = run_first_bags(blocks((side, across), half_a), got)
    a_got = lax.ppermute(a_sent, "grp", side_moves)
    b_sent = run_later_bags(blocks((opposite, across), half_b), prepared, "b_sent")
    b_got = lax.ppermute(b_sent, "grp", mirror_moves)
    a_kept = run_later_bags(blocks((me, opposite), half_a), prepared, "a_kept")
    part = ((2, *CHUNK), bf16)
    a_own, a_next = small_call(add_parts_kernel, "add_a", (part, part), a_kept, a_got)
    a_last = lax.ppermute(a_next, "grp", mirror_moves)
    b_blocks, a_own = lax.optimization_barrier((blocks((me, side), half_b), a_own))
    b_kept = run_later_bags(b_blocks, prepared, "b_kept")
    b_own, b_next = small_call(add_parts_kernel, "add_b", (part, part), b_kept, b_got)
    b_last = lax.ppermute(b_next, "grp", side_moves)
    chunk = (CHUNK, bf16)
    near, mirror = small_call(sum_a_kernel, "sum_a", (chunk, chunk), a_own, a_last)
    b_own, near, mirror = lax.optimization_barrier((b_own, near, mirror))
    near = lax.ppermute(near, "slot", swaps[1])
    mirror = lax.ppermute(mirror, "slot", swaps[3])
    kept, far = small_call(sum_b_kernel, "sum_b", ((CHUNK, f32), chunk), b_own, b_last)
    far = lax.ppermute(far, "slot", swaps[2])
    return small_call(final_kernel, "final_sum", ((CHUNK, f32),), kept, near, mirror, far)[0]


def solution(mesh):
    in_specs = (
        P(("dp", "grp"), "slot", None),
        P(("dp", "grp"), "slot", None),
        P(),
        P(),
        P(),
        P(),
        P(("dp", "grp"), "slot", None),
        P(("dp", "grp"), "slot"),
        P("slot"),
        P(),
    )
    out_specs = P("dp", ("slot", "grp"), None)
    return jax.shard_map(
        per_device, mesh=mesh, in_specs=in_specs, out_specs=out_specs, check_vma=False
    )
```
